128 devices in a mesh: expert: 128 (over x, z, y, core).
Axes of the slice: x: 4, y: 4, z: 4, core: 2. Of those that a mesh axis runs over, the one named last changes fastest.
Arguments:
- tokens: bfloat16 [8192, 2048], P('expert'), may hold values from -6 to 6
- expert_ids: int32 [8192, 8], P('expert'), may hold values from 0 to 127, as said below
- gate_scores: float32 [8192, 8], P('expert'), may hold values from 0.1 to 1
- w_gate: bfloat16 [128, 2048, 768], P('expert'), may hold values from -0.125 to 0.125
- w_up: bfloat16 [128, 2048, 768], P('expert'), may hold values from -0.125 to 0.125
- w_down: bfloat16 [128, 768, 2048], P('expert'), may hold values from -0.21875 to 0.21875
Outputs:
- mixed: bfloat16 [8192, 2048], P('expert')
The draws below stay inside these ranges and needn't reach their ends.
Inputs may be any that keep to these rules, and one draw needn't show every extreme that they name: `expert_ids`: each row names 8 different experts. One set of 3 experts, the same everywhere, each is named by exactly 18 rows of each device's block of 64 rows; each other expert is named by at most 4 rows of one device's block, and some expert reaches 4 in every block.
All inputs are finite; a program needn't handle non-finite values.
Results may differ from the reference program's by a relative error of at most 0.0058.
Values may be sent and summed in bfloat16 or wider, within the bound.
No kernel may reach another device: no remote copies, remote signals or barrier semaphores. Data moves between devices by JAX's collectives and lax.ppermute only.
A program may use at most 192 MiB of HBM per device.

```python
import math
import jax
import jax.numpy as jnp
from jax import lax

D = 2048
FF = 768
TOP = 8
HOT = 3
TOK_DEV = 64
EXPERTS = 128
TOKENS = 8192
MOST = 18


def draw_expert_ids(key, part):
    key = jax.random.fold_in(key, 11)
    hot_key, block_key = jax.random.split(key)
    order = jax.random.permutation(hot_key, EXPERTS).astype(jnp.int32)
    hot_set = order[:HOT]
    cold_set = order[HOT:]
    cold_total = EXPERTS - HOT
    slots = jnp.arange(TOP, dtype=jnp.int32)

    def one_block(bkey):
        first, second, third = jax.random.split(bkey, 3)
        ranks = jax.vmap(lambda kk: jax.random.permutation(kk, TOK_DEV))(jax.random.split(first, HOT))
        flags = (ranks < MOST).T
        hot_count = jnp.sum(flags.astype(jnp.int32), axis=1)
        hot_pos = jnp.cumsum(flags.astype(jnp.int32), axis=1) - 1
        match = flags[:, :, None] & (hot_pos[:, :, None] == slots[None, None, :])
        hot_here = jnp.sum(jnp.where(match, hot_set[None, :, None], 0), axis=1).astype(jnp.int32)
        cold_count = TOP - hot_count
        start = jnp.cumsum(cold_count) - cold_count
        running = start[:, None] + slots[None, :] - hot_count[:, None]
        cold_perm = jax.random.permutation(second, cold_total).astype(jnp.int32)
        cold_here = cold_set[cold_perm[jnp.mod(running, cold_total)]]
        chosen = jnp.where(slots[None, :] < hot_count[:, None], hot_here, cold_here)
        shuffle = jax.vmap(lambda kk: jax.random.permutation(kk, TOP))(jax.random.split(third, TOK_DEV))
        return jnp.take_along_axis(chosen, shuffle.astype(jnp.int32), axis=1)
    blocks = TOKENS // TOK_DEV
    drawn = jax.vmap(one_block)(jax.random.split(block_key, blocks))
    return drawn.reshape(TOKENS, TOP).astype(jnp.int32)


def block_scale(key, dims, cuts, low, largest):
    loudness = 1.0
    for dim, shards_of in cuts:
        steps = jax.random.uniform(jax.random.fold_in(jax.random.fold_in(key, 6), dim), (shards_of,), jnp.float32, low / len(cuts), largest / len(cuts))
        loudness = loudness * jnp.repeat(jnp.exp(steps), dims[dim] // shards_of).reshape((-1,) + (1,) * (len(dims) - 1 - dim))
    return loudness


def noise(rng, extent, spread, bound, cuts=(), kind=jnp.bfloat16):
    values = spread * jax.random.normal(rng, extent, jnp.float32)
    if cuts:
        values = values * block_scale(rng, extent, cuts, -0.22, 0.18)
    return jnp.clip(values, -bound, bound).astype(kind)


def setup_inputs(seed: int = 0) -> dict:
    key_of = jax.random.split(jax.random.key(seed), 7)
    tokens = noise(key_of[0], (TOKENS, D), 1.0, 6.0, ((0, 128),))
    expert_ids = draw_expert_ids(jax.random.fold_in(key_of[6], 71), 0)
    gate_scores = jnp.clip(jnp.exp(math.log(1.0) - 2.3025851 * jax.random.uniform(key_of[2], (TOKENS, TOP), jnp.float32) ** block_scale(key_of[2], (TOKENS, TOP), ((0, 128),), -0.2, 0.2)), 0.1, 1.0)
    w_gate = noise(key_of[3], (EXPERTS, D, FF), D ** -0.5, 0.125, ((0, 128),))
    w_up = noise(key_of[4], (EXPERTS, D, FF), D ** -0.5, 0.125, ((0, 128),))
    w_down = noise(key_of[5], (EXPERTS, FF, D), FF ** -0.5, 0.21875, ((0, 128),))
    return dict(tokens=tokens, expert_ids=expert_ids, gate_scores=gate_scores, w_gate=w_gate, w_up=w_up, w_down=w_down)


block_rows = 512


def expert_ffn(rows, gate_mat, up_mat, down_mat):
    gate_act = jnp.dot(rows, gate_mat, preferred_element_type=jnp.float32)
    upper = jnp.dot(rows, up_mat, preferred_element_type=jnp.float32)
    hidden = (jax.nn.silu(gate_act) * upper).astype(jnp.bfloat16)
    return jnp.dot(hidden, down_mat, preferred_element_type=jnp.float32).astype(jnp.bfloat16)


def reference(tokens, expert_ids, gate_scores, w_gate, w_up, w_down):
    weights = gate_scores / jnp.sum(gate_scores, axis=1, keepdims=True)
    flat_ids = expert_ids.reshape(-1).astype(jnp.int32)
    assigned = flat_ids.shape[0]
    model_width = tokens.shape[1]
    order = jnp.argsort(flat_ids, stable=True).astype(jnp.int32)
    expert_loads = jax.ops.segment_sum(jnp.ones((assigned,), jnp.int32), flat_ids, num_segments=EXPERTS).astype(jnp.int32)
    offsets = (jnp.cumsum(expert_loads) - expert_loads).astype(jnp.int32)
    token_of = (order // TOP).astype(jnp.int32)
    lane = jnp.arange(block_rows, dtype=jnp.int32)
    results = jnp.zeros((assigned, model_width), jnp.bfloat16)

    def per_expert(expert, results):
        expert = jnp.asarray(expert).astype(jnp.int32)
        needed = expert_loads[expert]

        def test_more(state):
            return state[0] * block_rows < needed

        def one_block(state):
            turn, results = state
            within = turn * block_rows + lane
            valid = within < needed
            position = (offsets[expert] + jnp.minimum(within, needed - 1)).astype(jnp.int32)
            chosen = tokens[token_of[position]]
            answer = expert_ffn(chosen, w_gate[expert], w_up[expert], w_down[expert])
            target = jnp.where(valid, position, assigned).astype(jnp.int32)
            results = results.at[target].set(answer, mode="drop")
            return turn + 1, results

        return lax.while_loop(test_more, one_block, (jnp.int32(0), results))[1]

    results = lax.fori_loop(0, EXPERTS, per_expert, results)
    placed = jnp.zeros_like(results).at[order].set(results).reshape(-1, TOP, model_width)
    summed = jnp.zeros((placed.shape[0], model_width), jnp.float32)
    for pick in range(TOP):
        summed = summed + weights[:, pick][:, None] * placed[:, pick, :].astype(jnp.float32)
    return summed.astype(jnp.bfloat16)
```

```python
import jax
import jax.numpy as jnp
from jax import lax
from jax.experimental import pallas as pl
from jax.experimental.pallas import tpu as pltpu
from jax.sharding import PartitionSpec as P

MOST = 18
BASE = 4
SPARE = 2
CAP = BASE + SPARE
HOT = 3
DIRS = ((0, 1), (0, -1), (1, 1), (1, -1), (2, 1), (2, -1))
F32 = jnp.float32
BF16 = jnp.bfloat16


def split_index(i):
    return (i >> 5) & 3, (i >> 3) & 3, (i >> 1) & 3


def moved_chip(i, axis, step):
    c = list(split_index(i))
    c[axis] = (c[axis] + step) & 3
    return (c[0] * 4 + c[1]) * 4 + c[2]


def hop_pairs(axis, step, n):
    return [(i, moved_chip(i, axis, step) * 2 + (i & 1)) for i in range(n)]


def plan_kernel(me_ref, ids_ref, tok_ref, out_ref, slot_ref, meta_ref):
    rows, picks = ids_ref.shape
    n = 128
    me = me_ref[0]
    lane = lax.broadcasted_iota(jnp.int32, (1, n), 1)
    lower = (
        lax.broadcasted_iota(jnp.int32, (rows, rows), 1)
        < lax.broadcasted_iota(jnp.int32, (rows, rows), 0)
    ).astype(BF16)
    upper = (
        lax.broadcasted_iota(jnp.int32, (n, n), 0) < lax.broadcasted_iota(jnp.int32, (n, n), 1)
    ).astype(BF16)

    def before_lane(flags):
        wide = jnp.broadcast_to(flags, (8, n)).astype(BF16)
        return jnp.dot(wide, upper, preferred_element_type=F32)[0:1]

    ids = ids_ref[...]
    lane_rows = lax.broadcasted_iota(jnp.int32, (rows, n), 1)
    run = jnp.zeros((1, n), F32)
    ranks, members = [], []
    for k in range(picks):
        member = (ids[:, k : k + 1] == lane_rows).astype(F32)
        ahead = jnp.dot(lower, member.astype(BF16), preferred_element_type=F32) + run
        ranks.append(jnp.sum(ahead * member, axis=1, keepdims=True).astype(jnp.int32))
        members.append(member)
        run = run + jnp.sum(member, axis=0, keepdims=True)
    hot = (run > BASE + 0.5).astype(F32)
    hot_rank = before_lane(hot)

    chips, near, same = [], [], []
    dev = split_index(lane)
    for h in range(HOT):
        mine = hot * (hot_rank == float(h)).astype(F32)
        where_hot = jnp.sum(lane.astype(F32) * mine, axis=1, keepdims=True).astype(jnp.int32)
        chips.append(where_hot >> 1)
        dist = jnp.zeros((1, n), jnp.int32)
        for a, b in zip(dev, split_index(where_hot)):
            gap = (a - b) & 3
            dist = dist + jnp.minimum(gap, 4 - gap)
        same.append((dist == 0).astype(F32))
        near.append((dist == 1).astype(F32))
    taken = jnp.minimum(same[0] + same[1] + same[2], 1.0)
    near = [v * (1.0 - taken) for v in near]
    avail, slot_of, order = [], [], []
    used = jnp.zeros((1, n), F32)
    ok = jnp.ones((1, 1), F32)
    for h in range(HOT):
        free = near[h] * (used < SPARE - 0.5).astype(F32)
        avail.append(free)
        slot_of.append(used)
        order.append(before_lane(free))
        used = used + free
        enough = jnp.sum(free, axis=1, keepdims=True) > MOST - CAP - SPARE - 0.5
        ok = ok * enough.astype(F32)
    for a, b in ((0, 1), (0, 2), (1, 2)):
        ok = ok * (chips[a] != chips[b]).astype(F32)

    slots_wide = lax.broadcasted_iota(jnp.int32, (rows, n * CAP), 1)
    lane_f = lane.astype(F32)
    chosen = jnp.zeros((rows, n * CAP), F32)
    slot_cols = []
    for k in range(picks):
        e, q, member = ids[:, k : k + 1], ranks[k], members[k]
        which = jnp.sum(member * (hot * (hot_rank + 1.0)), axis=1, keepdims=True)
        slot = jnp.where(q < CAP, e * CAP + q, (e ^ 1) * CAP + BASE + (q - CAP))
        far = jnp.zeros((rows, 1), F32)
        turn = (q - (CAP + SPARE)).astype(F32)
        for h in range(HOT):
            hit = avail[h] * (order[h] == turn).astype(F32) * (which == h + 1.0).astype(F32)
            far = far + jnp.sum(hit * (lane_f * CAP + BASE + slot_of[h]), axis=1, keepdims=True)
        slot = jnp.where(q < CAP + SPARE, slot, far.astype(jnp.int32))
        slot_cols.append(slot)
        chosen = chosen + (slot == slots_wide).astype(F32)
    slot_ref[...] = jnp.concatenate(slot_cols, axis=1)
    chosen = chosen.astype(BF16)
    out_ref[...] = lax.dot_general(
        chosen, tok_ref[...], (((0,), (0,)), ((), ())), preferred_element_type=F32
    ).astype(BF16)

    here = (lane == me).astype(F32)
    meta = jnp.zeros((1, n), F32)
    source = [jnp.zeros((1, n), F32) for _ in range(SPARE)]
    for d, (axis, step) in enumerate(DIRS):
        target = moved_chip(lane, axis, step)
        sent = jnp.zeros((1, n), F32)
        for h in range(HOT):
            serves = avail[h] * (target == chips[h]).astype(F32)
            sent = sent + serves * slot_of[h]
            for j in range(SPARE):
                source[j] = source[j] + serves * (slot_of[h] == float(j)).astype(F32) * (1.0 + d)
        meta = jnp.where(lane == d, jnp.sum(sent * here, axis=1, keepdims=True), meta)
    for j in range(SPARE):
        meta = jnp.where(lane == 6 + j, jnp.sum(source[j] * here, axis=1, keepdims=True), meta)
    meta = jnp.where(lane == 8, jnp.sum(hot * here, axis=1, keepdims=True), meta)
    meta = jnp.where(lane == 9, jnp.sum(taken * here, axis=1, keepdims=True), meta)
    meta = jnp.where(lane == 10, ok, meta)
    meta_ref[...] = meta.astype(jnp.int32)


def plan(me, ids, tokens):
    rows, width = tokens.shape
    vmem = pl.BlockSpec(memory_space=pltpu.VMEM)
    return pl.pallas_call(
        plan_kernel,
        in_specs=[pl.BlockSpec(memory_space=pltpu.SMEM), vmem, vmem],
        out_specs=[vmem, vmem, vmem],
        out_shape=[
            jax.ShapeDtypeStruct((128 * CAP, width), BF16),
            jax.ShapeDtypeStruct(ids.shape, jnp.int32),
            jax.ShapeDtypeStruct((1, 128), jnp.int32),
        ],
        compiler_params=pltpu.CompilerParams(vmem_limit_bytes=40 * 2**20),
        name="plan",
    )(me, ids, tokens)


def ffn_block(x_ref, out_ref, acc_ref, gate_ref, up_ref, down_ref, step, last, tile):
    @pl.loop(0, x_ref.shape[0] // tile)
    def _(i):
        at = pl.ds(pl.multiple_of(i * tile, tile), tile)
        x = x_ref[at, :]
        gate_act = jnp.dot(x, gate_ref[0], preferred_element_type=F32)
        upper = jnp.dot(x, up_ref[0], preferred_element_type=F32)
        hidden = (jax.nn.silu(gate_act) * upper).astype(BF16)
        part = jnp.dot(hidden, down_ref[0], preferred_element_type=F32)

        @pl.when(step == 0)
        def _():
            acc_ref[at, :] = part

        @pl.when((step > 0) & (step < last))
        def _():
            acc_ref[at, :] += part

        @pl.when(step == last)
        def _():
            out_ref[at, :] = (acc_ref[at, :] + part).astype(BF16)


def ffn_kernel(x_ref, gate_ref, up_ref, down_ref, out_ref, acc_ref):
    ffn_block(
        x_ref, out_ref, acc_ref, gate_ref, up_ref, down_ref,
        pl.program_id(0), pl.num_programs(0) - 1, 256,
    )


def ffn(x, gate_mat, up_mat, down_mat):
    rows, width = x.shape
    inner = gate_mat.shape[2]
    step = min(256, inner)
    return pl.pallas_call(
        ffn_kernel,
        grid=(inner // step,),
        in_specs=[
            pl.BlockSpec((rows, width), lambda f: (0, 0)),
            pl.BlockSpec((1, width, step), lambda f: (0, 0, f)),
            pl.BlockSpec((1, width, step), lambda f: (0, 0, f)),
            pl.BlockSpec((1, step, width), lambda f: (0, f, 0)),
        ],
        out_specs=pl.BlockSpec((rows, width), lambda f: (0, 0)),
        out_shape=jax.ShapeDtypeStruct((rows, width), BF16),
        scratch_shapes=[pltpu.VMEM((rows, width), F32)],
        compiler_params=pltpu.CompilerParams(vmem_limit_bytes=48 * 2**20),
        cost_estimate=pl.CostEstimate(
            flops=6 * rows * width * inner, bytes_accessed=6 * width * inner, transcendentals=0
        ),
        name="ffn",
    )(x, gate_mat, up_mat, down_mat)


def hot_kernel(flags_ref, x_ref, g0, u0, d0, g1, u1, d1, out_ref, acc_ref):
    step, last = pl.program_id(0), pl.num_programs(0) - 1

    @pl.when(flags_ref[8] == 1)
    def _():
        ffn_block(x_ref, out_ref, acc_ref, g0, u0, d0, step, last, 256)

    @pl.when((flags_ref[8] == 0) & (flags_ref[9] == 1))
    def _():
        ffn_block(x_ref, out_ref, acc_ref, g1, u1, d1, step, last, 256)

    @pl.when((flags_ref[9] == 0) & (step == last))
    def _():
        out_ref[...] = jnp.zeros_like(out_ref)


def hot_ffn(flags, x, own, other):
    rows, width = x.shape
    inner = own[0].shape[2]
    step = min(256, inner)

    def pick(f, flags, mine):
        use = flags[8] if mine else (1 - flags[8]) * flags[9]
        return f * use

    def across(mine):
        return pl.BlockSpec((1, width, step), lambda f, flags: (0, 0, pick(f, flags, mine)))

    def down(mine):
        return pl.BlockSpec((1, step, width), lambda f, flags: (0, pick(f, flags, mine), 0))

    whole = pl.BlockSpec((rows, width), lambda f, flags: (0, 0))
    return pl.pallas_call(
        hot_kernel,
        grid_spec=pltpu.PrefetchScalarGridSpec(
            num_scalar_prefetch=1,
            grid=(inner // step,),
            in_specs=[
                whole,
                across(True), across(True), down(True),
                across(False), across(False), down(False),
            ],
            out_specs=whole,
            scratch_shapes=[pltpu.VMEM((rows, width), F32)],
        ),
        out_shape=jax.ShapeDtypeStruct((rows, width), BF16),
        compiler_params=pltpu.CompilerParams(vmem_limit_bytes=52 * 2**20),
        cost_estimate=pl.CostEstimate(
            flops=6 * rows * width * inner, bytes_accessed=6 * width * inner, transcendentals=0
        ),
        name="hot_ffn",
    )(flags, x, *own, *other)


def mix_kernel(score_ref, slot_ref, ans_ref, out_ref):
    rows, picks = slot_ref.shape
    scores = score_ref[...]
    weights = scores / jnp.sum(scores, axis=1, keepdims=True)
    slots = slot_ref[...]
    wide = lax.broadcasted_iota(jnp.int32, (rows, ans_ref.shape[0]), 1)
    mix = jnp.zeros(wide.shape, F32)
    for k in range(picks):
        mix = jnp.where(slots[:, k : k + 1] == wide, weights[:, k : k + 1], mix)
    high = mix.astype(BF16)
    low = (mix - high.astype(F32)).astype(BF16)
    answers = ans_ref[...]
    out_ref[...] = (
        jnp.dot(high, answers, preferred_element_type=F32)
        + jnp.dot(low, answers, preferred_element_type=F32)
    ).astype(BF16)


def mix(scores, slots, answers):
    vmem = pl.BlockSpec(memory_space=pltpu.VMEM)
    return pl.pallas_call(
        mix_kernel,
        in_specs=[vmem, vmem, vmem],
        out_specs=vmem,
        out_shape=jax.ShapeDtypeStruct((slots.shape[0], answers.shape[1]), BF16),
        compiler_params=pltpu.CompilerParams(vmem_limit_bytes=40 * 2**20),
        name="mix",
    )(scores, slots, answers)


def exchange(x):
    n, slots, width = x.shape
    sent = x.reshape(n, slots * width // 128, 128)
    got = lax.all_to_all(sent, "expert", split_axis=0, concat_axis=0, tiled=True)
    return got.reshape(n, slots, width)


def relayed(tokens, ids, scores, w_gate, w_up, w_down, outgoing, slots, meta):
    n = lax.axis_size("expert")
    width = tokens.shape[1]
    flags = meta[0]
    swap = [(i, i ^ 1) for i in range(n)]
    own = (w_gate, w_up, w_down)
    other = tuple(lax.ppermute(w, "expert", swap) for w in own)
    got = exchange(outgoing.reshape(n, CAP, width))
    spare = [got[:, BASE + j] for j in range(SPARE)]
    hopped = [
        lax.ppermute(
            jnp.where(flags[d] == 0, spare[0], spare[1]), "expert", hop_pairs(axis, step, n)
        )
        for d, (axis, step) in enumerate(DIRS)
    ]
    served = ffn(got[:, :BASE].reshape(n * BASE, width), *own)
    hot_rows = hot_ffn(flags, jnp.concatenate(spare + hopped, axis=0), own, other)
    hot_rows = hot_rows.reshape(SPARE + len(DIRS), n, width)
    back = [
        lax.ppermute(hot_rows[SPARE + d], "expert", hop_pairs(axis, -step, n))
        for d, (axis, step) in enumerate(DIRS)
    ]
    answers = [served.reshape(n, BASE, width)]
    for j in range(SPARE):
        answer = hot_rows[j]
        for d in range(len(DIRS)):
            answer = jnp.where(flags[6 + j] == 1 + d, back[d], answer)
        answers.append(answer[:, None, :])
    answered = exchange(jnp.concatenate(answers, axis=1))
    return mix(scores, slots, answered.reshape(n * CAP, width))


def expert_ffn(rows, gate_mat, up_mat, down_mat):
    gate_act = jnp.dot(rows, gate_mat, preferred_element_type=F32)
    upper = jnp.dot(rows, up_mat, preferred_element_type=F32)
    hidden = (jax.nn.silu(gate_act) * upper).astype(BF16)
    return jnp.dot(hidden, down_mat, preferred_element_type=F32).astype(BF16)


def direct(tokens, ids, scores, w_gate, w_up, w_down, outgoing, slots, meta):
    rows, picks = ids.shape
    n = lax.axis_size("expert")
    width = tokens.shape[1]
    weights = scores / jnp.sum(scores, axis=1, keepdims=True)
    flat = ids.reshape(-1)
    experts = jnp.arange(n, dtype=jnp.int32)
    member = (flat[:, None] == experts[None, :]).astype(jnp.int32)
    before = jnp.cumsum(member, axis=0) - member
    target = flat * MOST + jnp.sum(before * member, axis=1)
    sent = jnp.zeros((n * MOST, width), BF16).at[target].set(jnp.repeat(tokens, picks, axis=0))
    got = exchange(sent.reshape(n, MOST, width))
    served = expert_ffn(got.reshape(n * MOST, width), w_gate[0], w_up[0], w_down[0])
    answered = exchange(served.reshape(n, MOST, width)).reshape(n * MOST, width)
    picked = weights.reshape(-1)[:, None] * answered[target].astype(F32)
    return jnp.sum(picked.reshape(rows, picks, width), axis=1).astype(BF16)


def body(tokens, ids, scores, w_gate, w_up, w_down):
    me = lax.axis_index("expert").astype(jnp.int32).reshape(1)
    outgoing, slots, meta = plan(me, ids, tokens)
    return lax.cond(
        meta[0, 10] == 1, relayed, direct,
        tokens, ids, scores, w_gate, w_up, w_down, outgoing, slots, meta,
    )


def solution(mesh):
    placed = (
        P("expert", None),
        P("expert", None),
        P("expert", None),
        P("expert", None, None),
        P("expert", None, None),
        P("expert", None, None),
    )
    return jax.shard_map(
        body, mesh=mesh, in_specs=placed, out_specs=P("expert", None), check_vma=False
    )
```

```python
import jax
import jax.numpy as jnp
from jax import lax
from jax.experimental import pallas as pl
from jax.experimental.pallas import tpu as pltpu
from jax.sharding import PartitionSpec as P

MOST = 18
BASE = 4
SPARE = 2
CAP = BASE + SPARE
HOT = 3
LINES = 16
DIRS = ((0, 1), (0, -1), (1, 1), (1, -1), (2, 1), (2, -1))
F32 = jnp.float32
BF16 = jnp.bfloat16


def split_index(i):
    return (i >> 5) & 3, (i >> 3) & 3, (i >> 1) & 3


def moved_chip(i, axis, step):
    c = list(split_index(i))
    c[axis] = (c[axis] + step) & 3
    return (c[0] * 4 + c[1]) * 4 + c[2]


def hop_pairs(axis, step, n):
    return [(i, moved_chip(i, axis, step) * 2 + (i & 1)) for i in range(n)]


def plan_kernel(me_ref, ids_ref, tok_ref, out_ref, slot_ref, meta_ref, wide_ref):
    rows, picks = ids_ref.shape
    n = 128
    me = me_ref[0]
    lane = lax.broadcasted_iota(jnp.int32, (1, n), 1)
    lower = (
        lax.broadcasted_iota(jnp.int32, (rows, rows), 1)
        < lax.broadcasted_iota(jnp.int32, (rows, rows), 0)
    ).astype(BF16)
    upper = (
        lax.broadcasted_iota(jnp.int32, (n, n), 0) < lax.broadcasted_iota(jnp.int32, (n, n), 1)
    ).astype(BF16)

    def before_lane(flags):
        wide = jnp.broadcast_to(flags, (8, n)).astype(BF16)
        return jnp.dot(wide, upper, preferred_element_type=F32)[0:1]

    ids = ids_ref[...]
    lane_rows = lax.broadcasted_iota(jnp.int32, (rows, n), 1)
    run = jnp.zeros((1, n), F32)
    ranks, members = [], []
    for k in range(picks):
        member = (ids[:, k : k + 1] == lane_rows).astype(F32)
        ahead = jnp.dot(lower, member.astype(BF16), preferred_element_type=F32) + run
        ranks.append(jnp.sum(ahead * member, axis=1, keepdims=True).astype(jnp.int32))
        members.append(member)
        run = run + jnp.sum(member, axis=0, keepdims=True)
    hot = (run > BASE + 0.5).astype(F32)
    hot_rank = before_lane(hot)

    chips, near, same = [], [], []
    dev = split_index(lane)
    for h in range(HOT):
        mine = hot * (hot_rank == float(h)).astype(F32)
        where_hot = jnp.sum(lane.astype(F32) * mine, axis=1, keepdims=True).astype(jnp.int32)
        chips.append(where_hot >> 1)
        dist = jnp.zeros((1, n), jnp.int32)
        for a, b in zip(dev, split_index(where_hot)):
            gap = (a - b) & 3
            dist = dist + jnp.minimum(gap, 4 - gap)
        same.append((dist == 0).astype(F32))
        near.append((dist == 1).astype(F32))
    taken = jnp.minimum(same[0] + same[1] + same[2], 1.0)
    near = [v * (1.0 - taken) for v in near]
    avail, slot_of, order = [], [], []
    used = jnp.zeros((1, n), F32)
    ok = jnp.ones((1, 1), F32)
    for h in range(HOT):
        free = near[h] * (used < SPARE - 0.5).astype(F32)
        avail.append(free)
        slot_of.append(used)
        order.append(before_lane(free))
        used = used + free
        enough = jnp.sum(free, axis=1, keepdims=True) > MOST - CAP - SPARE - 0.5
        ok = ok * enough.astype(F32)
    for a, b in ((0, 1), (0, 2), (1, 2)):
        ok = ok * (chips[a] != chips[b]).astype(F32)

    slots_wide = lax.broadcasted_iota(jnp.int32, (rows, n * CAP), 1)
    lane_f = lane.astype(F32)
    chosen = jnp.zeros((rows, n * CAP), F32)
    slot_cols = []
    for k in range(picks):
        e, q, member = ids[:, k : k + 1], ranks[k], members[k]
        which = jnp.sum(member * (hot * (hot_rank + 1.0)), axis=1, keepdims=True)
        code = jnp.where(q < CAP, e * 8 + q, (e ^ 1) * 8 + BASE + (q - CAP))
        far = jnp.zeros((rows, 1), F32)
        turn = (q - (CAP + SPARE)).astype(F32)
        for h in range(HOT):
            hit = avail[h] * (order[h] == turn).astype(F32) * (which == h + 1.0).astype(F32)
            far = far + jnp.sum(hit * (lane_f * 8 + BASE + slot_of[h]), axis=1, keepdims=True)
        code = jnp.where(q < CAP + SPARE, code, far.astype(jnp.int32))
        place, turn = code >> 3, code & 7
        slot_cols.append(
            jnp.where(turn < BASE, place * BASE + turn, n * BASE + place * SPARE + turn - BASE)
        )
        chosen = chosen + (place * CAP + turn == slots_wide).astype(F32)
    slot_ref[...] = jnp.concatenate(slot_cols, axis=1)
    chosen = chosen.astype(BF16)
    for c in range(tok_ref.shape[1] // 256):
        picked = lax.dot_general(
            chosen, tok_ref[:, c * 256 : (c + 1) * 256], (((0,), (0,)), ((), ())),
            preferred_element_type=F32,
        )
        for j in range(2):
            wide_ref[pl.ds(2 * c + j, n * CAP, stride=LINES), :] = picked[:, j * 128 : (j + 1) * 128]
    out_ref[...] = wide_ref[...].astype(BF16)

    here = (lane == me).astype(F32)
    meta = jnp.zeros((1, n), F32)
    source = [jnp.zeros((1, n), F32) for _ in range(SPARE)]
    for d, (axis, step) in enumerate(DIRS):
        target = moved_chip(lane, axis, step)
        sent = jnp.zeros((1, n), F32)
        for h in range(HOT):
            serves = avail[h] * (target == chips[h]).astype(F32)
            sent = sent + serves * slot_of[h]
            for j in range(SPARE):
                source[j] = source[j] + serves * (slot_of[h] == float(j)).astype(F32) * (1.0 + d)
        meta = jnp.where(lane == d, jnp.sum(sent * here, axis=1, keepdims=True), meta)
    for j in range(SPARE):
        meta = jnp.where(lane == 6 + j, jnp.sum(source[j] * here, axis=1, keepdims=True), meta)
    meta = jnp.where(lane == 8, jnp.sum(hot * here, axis=1, keepdims=True), meta)
    meta = jnp.where(lane == 9, jnp.sum(taken * here, axis=1, keepdims=True), meta)
    meta = jnp.where(lane == 10, ok, meta)
    meta_ref[...] = meta.astype(jnp.int32)


def plan(me, ids, tokens):
    rows, width = tokens.shape
    vmem = pl.BlockSpec(memory_space=pltpu.VMEM)
    return pl.pallas_call(
        plan_kernel,
        in_specs=[pl.BlockSpec(memory_space=pltpu.SMEM), vmem, vmem],
        out_specs=[vmem, vmem, vmem],
        out_shape=[
            jax.ShapeDtypeStruct((128 * CAP * LINES, 128), BF16),
            jax.ShapeDtypeStruct(ids.shape, jnp.int32),
            jax.ShapeDtypeStruct((1, 128), jnp.int32),
        ],
        scratch_shapes=[pltpu.VMEM((128 * CAP * LINES, 128), F32)],
        compiler_params=pltpu.CompilerParams(vmem_limit_bytes=40 * 2**20),
        name="plan",
    )(me, ids, tokens)


UP_STEPS = 3
DOWN_STEPS = 4


def unpack(packed, lines_ref, x_ref, group):
    lines_ref[...] = packed.astype(F32)
    rows = packed.shape[0] // LINES
    for j in range(LINES):
        line = lines_ref[pl.ds(j, rows, stride=LINES), :]
        x_ref[group * rows : (group + 1) * rows, j * 128 : (j + 1) * 128] = line.astype(BF16)


def ffn_steps(load, store, groups, gate_ref, up_ref, down_ref, x_ref, lines_ref, hid_ref, wide_ref):
    step = pl.program_id(0)
    rows = x_ref.shape[0]
    tile = 512
    per = rows // groups

    @pl.when(step == 0)
    def _():
        for g in range(groups):
            unpack(load(g), lines_ref, x_ref, g)

    @pl.when(step < UP_STEPS)
    def _():
        @pl.loop(0, rows // tile)
        def _(i):
            at = pl.ds(pl.multiple_of(i * tile, tile), tile)
            x = x_ref[at, :]
            gate_act = jnp.dot(x, gate_ref[0], preferred_element_type=F32)
            upper = jnp.dot(x, up_ref[0], preferred_element_type=F32)
            hid_ref[step, at, :] = (jax.nn.silu(gate_act) * upper).astype(BF16)

    @pl.when(step >= UP_STEPS)
    def _():
        width = down_ref.shape[2]
        inner = hid_ref.shape[2]

        @pl.loop(0, rows // tile)
        def _(i):
            at = pl.ds(pl.multiple_of(i * tile, tile), tile)
            part = jnp.dot(hid_ref[0, at, :], down_ref[0, :inner], preferred_element_type=F32)
            for p in range(1, UP_STEPS):
                part += jnp.dot(
                    hid_ref[p, at, :], down_ref[0, p * inner : (p + 1) * inner],
                    preferred_element_type=F32,
                )
            for j in range(width // 128):
                line = (step - UP_STEPS) * (width // 128) + j
                wide_ref[pl.ds(i * (tile * LINES) + line, tile, stride=LINES), :] = part[
                    :, j * 128 : (j + 1) * 128
                ]

    @pl.when(step == UP_STEPS + DOWN_STEPS - 1)
    def _():
        for g in range(groups):
            store(g, wide_ref[g * per * LINES : (g + 1) * per * LINES, :].astype(BF16))


def ffn_scratch(rows, per, width, inner):
    return [
        pltpu.VMEM((rows, width), BF16),
        pltpu.VMEM((per * LINES, 128), F32),
        pltpu.VMEM((UP_STEPS, rows, inner // UP_STEPS), BF16),
        pltpu.VMEM((rows * LINES, 128), F32),
    ]


def ffn_cost(rows, width, inner):
    return pl.CostEstimate(
        flops=6 * rows * width * inner, bytes_accessed=6 * width * inner, transcendentals=0
    )


def ffn_kernel(x_ref, gate_ref, up_ref, down_ref, out_ref, *scratch):
    n = x_ref.shape[0]

    def load(g):
        return x_ref[:, g * LINES : (g + 1) * LINES, :].reshape(n * LINES, 128)

    def store(g, lines):
        out_ref[:, g * LINES : (g + 1) * LINES, :] = lines.reshape(n, LINES, 128)

    ffn_steps(load, store, BASE, gate_ref, up_ref, down_ref, *scratch)


def ffn(x, gate_mat, up_mat, down_mat):
    n = x.shape[0]
    width, inner = gate_mat.shape[1:]
    rows = n * BASE
    return pl.pallas_call(
        ffn_kernel,
        grid=(UP_STEPS + DOWN_STEPS,),
        in_specs=[
            pl.BlockSpec(x.shape, lambda f: (0, 0, 0)),
            pl.BlockSpec((1, width, inner // UP_STEPS), lambda f: (0, 0, jnp.minimum(f, UP_STEPS - 1))),
            pl.BlockSpec((1, width, inner // UP_STEPS), lambda f: (0, 0, jnp.minimum(f, UP_STEPS - 1))),
            pl.BlockSpec((1, inner, width // DOWN_STEPS), lambda f: (0, 0, jnp.maximum(f - UP_STEPS, 0))),
        ],
        out_specs=pl.BlockSpec((n, BASE * LINES, 128), lambda f: (0, 0, 0)),
        out_shape=jax.ShapeDtypeStruct((n, BASE * LINES, 128), BF16),
        scratch_shapes=ffn_scratch(rows, n, width, inner),
        compiler_params=pltpu.CompilerParams(vmem_limit_bytes=48 * 2**20),
        cost_estimate=ffn_cost(rows, width, inner),
        name="ffn",
    )(x, gate_mat, up_mat, down_mat)


GROUPS = SPARE + len(DIRS)


def hot_kernel(flags_ref, *refs):
    xs, refs = refs[:GROUPS], refs[GROUPS:]
    own, refs = refs[:3], refs[3:]
    other, refs = refs[:3], refs[3:]
    outs, scratch = refs[:GROUPS], refs[GROUPS:]

    def load(g):
        return xs[g][...]

    def store(g, lines):
        outs[g][...] = lines

    @pl.when(flags_ref[8] == 1)
    def _():
        ffn_steps(load, store, GROUPS, *own, *scratch)

    @pl.when((flags_ref[8] == 0) & (flags_ref[9] == 1))
    def _():
        ffn_steps(load, store, GROUPS, *other, *scratch)

    @pl.when((flags_ref[9] == 0) & (pl.program_id(0) == 0))
    def _():
        for out in outs:
            out[...] = jnp.zeros_like(out)


def hot_ffn(flags, xs, own, other):
    lines = xs[0].shape[0]
    n = lines // LINES
    width, inner = own[0].shape[1:]
    rows = n * GROUPS

    def use(flags, mine):
        return flags[8] if mine else (1 - flags[8]) * flags[9]

    def across(mine):
        return pl.BlockSpec(
            (1, width, inner // UP_STEPS),
            lambda f, flags: (0, 0, jnp.minimum(f, UP_STEPS - 1) * use(flags, mine)),
        )

    def down(mine):
        return pl.BlockSpec(
            (1, inner, width // DOWN_STEPS),
            lambda f, flags: (0, 0, jnp.maximum(f - UP_STEPS, 0) * use(flags, mine)),
        )

    whole = pl.BlockSpec((lines, 128), lambda f, flags: (0, 0))
    return pl.pallas_call(
        hot_kernel,
        grid_spec=pltpu.PrefetchScalarGridSpec(
            num_scalar_prefetch=1,
            grid=(UP_STEPS + DOWN_STEPS,),
            in_specs=[whole] * GROUPS
            + [across(True), across(True), down(True), across(False), across(False), down(False)],
            out_specs=[whole] * GROUPS,
            scratch_shapes=ffn_scratch(rows, n, width, inner),
        ),
        out_shape=[jax.ShapeDtypeStruct((lines, 128), BF16)] * GROUPS,
        compiler_params=pltpu.CompilerParams(vmem_limit_bytes=56 * 2**20),
        cost_estimate=ffn_cost(rows, width, inner),
        name="hot_ffn",
    )(flags, *xs, *own, *other)


def mix_kernel(score_ref, slot_ref, base_ref, spare_ref, out_ref, lines_ref):
    rows, picks = slot_ref.shape
    n = base_ref.shape[0]
    cut = n * BASE * LINES
    lines_ref[:cut, :] = base_ref[...].reshape(cut, 128).astype(F32)
    lines_ref[cut:, :] = spare_ref[...].reshape(n * SPARE * LINES, 128).astype(F32)
    scores = score_ref[...]
    weights = scores / jnp.sum(scores, axis=1, keepdims=True)
    slots = slot_ref[...]
    wide = lax.broadcasted_iota(jnp.int32, (rows, n * CAP), 1)
    mix = jnp.zeros(wide.shape, F32)
    for k in range(picks):
        mix = jnp.where(slots[:, k : k + 1] == wide, weights[:, k : k + 1], mix)
    high = mix.astype(BF16)
    low = (mix - high.astype(F32)).astype(BF16)
    both = jnp.concatenate([high, low], axis=0)
    for j in range(LINES):
        answers = lines_ref[pl.ds(j, n * CAP, stride=LINES), :].astype(BF16)
        part = jnp.dot(both, answers, preferred_element_type=F32)
        out_ref[:, j * 128 : (j + 1) * 128] = (part[:rows] + part[rows:]).astype(BF16)


def mix(scores, slots, base, spare):
    n = base.shape[0]
    vmem = pl.BlockSpec(memory_space=pltpu.VMEM)
    return pl.pallas_call(
        mix_kernel,
        in_specs=[vmem] * 4,
        out_specs=vmem,
        out_shape=jax.ShapeDtypeStruct((slots.shape[0], LINES * 128), BF16),
        scratch_shapes=[pltpu.VMEM((n * CAP * LINES, 128), F32)],
        compiler_params=pltpu.CompilerParams(vmem_limit_bytes=40 * 2**20),
        name="mix",
    )(scores, slots, base, spare)


def exchange(x):
    return lax.all_to_all(x, "expert", split_axis=0, concat_axis=0, tiled=True)


def relayed(scores, w_gate, w_up, w_down, outgoing, slots, meta):
    n = lax.axis_size("expert")
    flags = meta[0]
    swap = [(i, i ^ 1) for i in range(n)]
    own = (w_gate, w_up, w_down)
    other = [lax.ppermute(w, "expert", swap) for w in own]
    got, *other = lax.optimization_barrier((exchange(outgoing), *other))
    spare = [
        got[:, (BASE + j) * LINES : (BASE + j + 1) * LINES].reshape(n * LINES, 128)
        for j in range(SPARE)
    ]
    hopped = [
        lax.ppermute(
            jnp.where(flags[d] == 0, spare[0], spare[1]), "expert", hop_pairs(axis, step, n)
        )
        for d, (axis, step) in enumerate(DIRS)
    ]
    served, *hopped = lax.optimization_barrier((ffn(got, *own), *hopped))
    base = exchange(served)
    hot_rows = hot_ffn(flags, spare + hopped, own, other)
    back = [
        lax.ppermute(hot_rows[SPARE + d], "expert", hop_pairs(axis, -step, n))
        for d, (axis, step) in enumerate(DIRS)
    ]
    answers = []
    for j in range(SPARE):
        answer = hot_rows[j]
        for d in range(len(DIRS)):
            answer = jnp.where(flags[6 + j] == 1 + d, back[d], answer)
        answers.append(answer.reshape(n, LINES, 128))
    spare_back = exchange(jnp.concatenate(answers, axis=1))
    return mix(scores, slots, base, spare_back)


def expert_ffn(rows, gate_mat, up_mat, down_mat):
    gate_act = jnp.dot(rows, gate_mat, preferred_element_type=F32)
    upper = jnp.dot(rows, up_mat, preferred_element_type=F32)
    hidden = (jax.nn.silu(gate_act) * upper).astype(BF16)
    return jnp.dot(hidden, down_mat, preferred_element_type=F32).astype(BF16)


def direct(tokens, ids, scores, w_gate, w_up, w_down):
    rows, picks = ids.shape
    n = lax.axis_size("expert")
    width = tokens.shape[1]
    weights = scores / jnp.sum(scores, axis=1, keepdims=True)
    flat = ids.reshape(-1)
    experts = jnp.arange(n, dtype=jnp.int32)
    member = (flat[:, None] == experts[None, :]).astype(jnp.int32)
    before = jnp.cumsum(member, axis=0) - member
    target = flat * MOST + jnp.sum(before * member, axis=1)
    sent = jnp.zeros((n * MOST, width), BF16).at[target].set(jnp.repeat(tokens, picks, axis=0))
    got = exchange(sent.reshape(n, MOST * LINES, 128))
    served = expert_ffn(got.reshape(n * MOST, width), w_gate[0], w_up[0], w_down[0])
    answered = exchange(served.reshape(n, MOST * LINES, 128)).reshape(n * MOST, width)
    picked = weights.reshape(-1)[:, None] * answered[target].astype(F32)
    return jnp.sum(picked.reshape(rows, picks, width), axis=1).astype(BF16)


def body(tokens, ids, scores, w_gate, w_up, w_down):
    n = lax.axis_size("expert")
    me = lax.axis_index("expert").astype(jnp.int32).reshape(1)
    outgoing, slots, meta = plan(me, ids, tokens)
    mixed = relayed(
        scores, w_gate, w_up, w_down, outgoing.reshape(n, CAP * LINES, 128), slots, meta
    )
    return lax.cond(
        meta[0, 10] == 1,
        lambda mixed, *rest: mixed,
        lambda mixed, *rest: direct(*rest),
        mixed, tokens, ids, scores, w_gate, w_up, w_down,
    )


def solution(mesh):
    placed = (
        P("expert", None),
        P("expert", None),
        P("expert", None),
        P("expert", None, None),
        P("expert", None, None),
        P("expert", None, None),
    )
    return jax.shard_map(
        body, mesh=mesh, in_specs=placed, out_specs=P("expert", None), check_vma=False
    )
```

```python
import jax
import jax.numpy as jnp
from jax import lax
from jax.experimental import pallas as pl
from jax.experimental.pallas import tpu as pltpu
from jax.sharding import PartitionSpec as P

MOST = 18
BASE = 4
SPARE = 2
CAP = BASE + SPARE
HOT = 3
LINES = 16
DIRS = ((0, 1), (0, -1), (1, 1), (1, -1), (2, 1), (2, -1))
F32 = jnp.float32
BF16 = jnp.bfloat16


def split_index(i):
    return (i >> 5) & 3, (i >> 3) & 3, (i >> 1) & 3


def moved_chip(i, axis, step):
    c = list(split_index(i))
    c[axis] = (c[axis] + step) & 3
    return (c[0] * 4 + c[1]) * 4 + c[2]


def hop_pairs(axis, step, n):
    return [(i, moved_chip(i, axis, step) * 2 + (i & 1)) for i in range(n)]


def plan_kernel(me_ref, ids_ref, tok_ref, base_ref, spare_ref, slot_ref, meta_ref):
    rows, picks = ids_ref.shape
    n = 128
    me = me_ref[0]
    lane = lax.broadcasted_iota(jnp.int32, (1, n), 1)
    lower = (
        lax.broadcasted_iota(jnp.int32, (rows, rows), 1)
        < lax.broadcasted_iota(jnp.int32, (rows, rows), 0)
    ).astype(BF16)
    upper = (
        lax.broadcasted_iota(jnp.int32, (n, n), 0) < lax.broadcasted_iota(jnp.int32, (n, n), 1)
    ).astype(BF16)

    def before_lane(flags):
        wide = jnp.broadcast_to(flags, (8, n)).astype(BF16)
        return jnp.dot(wide, upper, preferred_element_type=F32)[0:1]

    ids = ids_ref[...]
    lane_rows = lax.broadcasted_iota(jnp.int32, (rows, n), 1)
    run = jnp.zeros((1, n), F32)
    ranks, members = [], []
    for k in range(picks):
        member = (ids[:, k : k + 1] == lane_rows).astype(F32)
        ahead = jnp.dot(lower, member.astype(BF16), preferred_element_type=F32) + run
        ranks.append(jnp.sum(ahead * member, axis=1, keepdims=True).astype(jnp.int32))
        members.append(member)
        run = run + jnp.sum(member, axis=0, keepdims=True)
    hot = (run > BASE + 0.5).astype(F32)
    hot_rank = before_lane(hot)

    chips, near, same = [], [], []
    dev = split_index(lane)
    for h in range(HOT):
        mine = hot * (hot_rank == float(h)).astype(F32)
        where_hot = jnp.sum(lane.astype(F32) * mine, axis=1, keepdims=True).astype(jnp.int32)
        chips.append(where_hot >> 1)
        dist = jnp.zeros((1, n), jnp.int32)
        for a, b in zip(dev, split_index(where_hot)):
            gap = (a - b) & 3
            dist = dist + jnp.minimum(gap, 4 - gap)
        same.append((dist == 0).astype(F32))
        near.append((dist == 1).astype(F32))
    taken = jnp.minimum(same[0] + same[1] + same[2], 1.0)
    near = [v * (1.0 - taken) for v in near]
    avail, slot_of, order = [], [], []
    used = jnp.zeros((1, n), F32)
    ok = jnp.ones((1, 1), F32)
    for h in range(HOT):
        free = near[h] * (used < SPARE - 0.5).astype(F32)
        avail.append(free)
        slot_of.append(used)
        order.append(before_lane(free))
        used = used + free
        enough = jnp.sum(free, axis=1, keepdims=True) > MOST - CAP - SPARE - 0.5
        ok = ok * enough.astype(F32)
    for a, b in ((0, 1), (0, 2), (1, 2)):
        ok = ok * (chips[a] != chips[b]).astype(F32)

    base_wide = lax.broadcasted_iota(jnp.int32, (rows, n * BASE), 1)
    spare_wide = lax.broadcasted_iota(jnp.int32, (rows, n * SPARE), 1)
    lane_f = lane.astype(F32)
    chosen_base = jnp.zeros(base_wide.shape, F32)
    chosen_spare = jnp.zeros(spare_wide.shape, F32)
    slot_cols = []
    for k in range(picks):
        e, q, member = ids[:, k : k + 1], ranks[k], members[k]
        which = jnp.sum(member * (hot * (hot_rank + 1.0)), axis=1, keepdims=True)
        code = jnp.where(q < CAP, e * 8 + q, (e ^ 1) * 8 + BASE + (q - CAP))
        far = jnp.zeros((rows, 1), F32)
        turn = (q - (CAP + SPARE)).astype(F32)
        for h in range(HOT):
            hit = avail[h] * (order[h] == turn).astype(F32) * (which == h + 1.0).astype(F32)
            far = far + jnp.sum(hit * (lane_f * 8 + BASE + slot_of[h]), axis=1, keepdims=True)
        code = jnp.where(q < CAP + SPARE, code, far.astype(jnp.int32))
        slot_cols.append(code)
        place, turn = code >> 3, code & 7
        at = jnp.where(turn < BASE, place * BASE + turn, -1)
        chosen_base = chosen_base + (at == base_wide).astype(F32)
        at = jnp.where(turn < BASE, -1, place * SPARE + turn - BASE)
        chosen_spare = chosen_spare + (at == spare_wide).astype(F32)
    slot_ref[...] = jnp.concatenate(slot_cols, axis=1)
    for chosen, out_ref in ((chosen_spare, spare_ref), (chosen_base, base_ref)):
        picked = lax.dot_general(
            chosen.astype(BF16), tok_ref[...], (((0,), (0,)), ((), ())),
            preferred_element_type=F32,
        )
        out_ref[...] = picked.astype(BF16).reshape(out_ref.shape)

    here = (lane == me).astype(F32)
    meta = jnp.zeros((1, n), F32)
    source = [jnp.zeros((1, n), F32) for _ in range(SPARE)]
    for d, (axis, step) in enumerate(DIRS):
        target = moved_chip(lane, axis, step)
        sent = jnp.zeros((1, n), F32)
        for h in range(HOT):
            serves = avail[h] * (target == chips[h]).astype(F32)
            sent = sent + serves * slot_of[h]
            for j in range(SPARE):
                source[j] = source[j] + serves * (slot_of[h] == float(j)).astype(F32) * (1.0 + d)
        meta = jnp.where(lane == d, jnp.sum(sent * here, axis=1, keepdims=True), meta)
    for j in range(SPARE):
        meta = jnp.where(lane == 6 + j, jnp.sum(source[j] * here, axis=1, keepdims=True), meta)
    meta = jnp.where(lane == 8, jnp.sum(hot * here, axis=1, keepdims=True), meta)
    meta = jnp.where(lane == 9, jnp.sum(taken * here, axis=1, keepdims=True), meta)
    meta = jnp.where(lane == 10, ok, meta)
    meta_ref[...] = meta.astype(jnp.int32)


def plan(me, ids, tokens):
    rows, width = tokens.shape
    vmem = pl.BlockSpec(memory_space=pltpu.VMEM)
    return pl.pallas_call(
        plan_kernel,
        in_specs=[pl.BlockSpec(memory_space=pltpu.SMEM), vmem, vmem],
        out_specs=[vmem] * 4,
        out_shape=[
            jax.ShapeDtypeStruct((128, BASE, width), BF16),
            jax.ShapeDtypeStruct((128, SPARE, width), BF16),
            jax.ShapeDtypeStruct(ids.shape, jnp.int32),
            jax.ShapeDtypeStruct((1, 128), jnp.int32),
        ],
        compiler_params=pltpu.CompilerParams(vmem_limit_bytes=32 * 2**20),
        name="plan",
    )(me, ids, tokens)


VMEM = pl.BlockSpec(memory_space=pltpu.VMEM)
SMEM = pl.BlockSpec(memory_space=pltpu.SMEM)
BLOCK = 256


def spread_kernel(flags_ref, got_ref, *refs):
    outs = refs
    n, spare, width = got_ref.shape
    got = got_ref[...].reshape(n * spare, width)
    row = lax.broadcasted_iota(jnp.int32, (n, n * spare), 0)
    column = lax.broadcasted_iota(jnp.int32, (n, n * spare), 1)
    for s in range(SPARE):
        take = (row * spare + s == column).astype(BF16)
        outs[s][...] = jnp.dot(take, got, preferred_element_type=F32).astype(BF16)
    for d in range(len(DIRS)):
        for s in range(SPARE):
            @pl.when(flags_ref[d] == s)
            def _():
                outs[SPARE + d][...] = outs[s][...]


def spread(flags, got):
    n, spare, width = got.shape
    return pl.pallas_call(
        spread_kernel,
        in_specs=[SMEM, VMEM],
        out_specs=[VMEM] * (SPARE + len(DIRS)),
        out_shape=[jax.ShapeDtypeStruct((n, width), BF16)] * (SPARE + len(DIRS)),
        compiler_params=pltpu.CompilerParams(vmem_limit_bytes=24 * 2**20),
        name="spread",
    )(flags, got)


def ffn_rows(x_ref, out_ref, hid_ref, gate_ref, up_ref, down_ref):
    blocks = hid_ref.shape[0]
    for p in range(blocks):
        at = slice(p * BLOCK, (p + 1) * BLOCK)
        x = x_ref[...]
        gate_act = jnp.dot(x, gate_ref[0, :, at], preferred_element_type=F32)
        upper = jnp.dot(x, up_ref[0, :, at], preferred_element_type=F32)
        hid_ref[p] = (jax.nn.silu(gate_act) * upper).astype(BF16)
    for c in range(x_ref.shape[1] // 512):
        at = slice(c * 512, (c + 1) * 512)
        part = jnp.dot(hid_ref[0], down_ref[0, :BLOCK, at], preferred_element_type=F32)
        for p in range(1, blocks):
            part += jnp.dot(
                hid_ref[p], down_ref[0, p * BLOCK : (p + 1) * BLOCK, at],
                preferred_element_type=F32,
            )
        out_ref[:, at] = part.astype(BF16)


def ffn_scratch(rows, width, inner):
    return [pltpu.VMEM((rows, width), BF16), pltpu.VMEM((inner // BLOCK, rows, BLOCK), BF16)]


def ffn_cost(rows, width, inner):
    return pl.CostEstimate(
        flops=6 * rows * width * inner, bytes_accessed=6 * width * inner, transcendentals=0
    )


def ffn_kernel(x_ref, gate_ref, up_ref, down_ref, out_ref, rows_ref, hid_ref):
    rows_ref[...] = x_ref[...].reshape(rows_ref.shape)
    ffn_rows(rows_ref, out_ref, hid_ref, gate_ref, up_ref, down_ref)


def ffn(x, gate_mat, up_mat, down_mat):
    n, slots, width = x.shape
    inner = gate_mat.shape[2]
    rows = n * slots
    return pl.pallas_call(
        ffn_kernel,
        in_specs=[VMEM] * 4,
        out_specs=VMEM,
        out_shape=jax.ShapeDtypeStruct((rows, width), BF16),
        scratch_shapes=ffn_scratch(rows, width, inner),
        compiler_params=pltpu.CompilerParams(vmem_limit_bytes=32 * 2**20),
        cost_estimate=ffn_cost(rows, width, inner),
        name="ffn",
    )(x, gate_mat, up_mat, down_mat)


def hot_kernel(flags_ref, *refs):
    groups = (len(refs) - 9) // 2
    xs, refs = refs[:groups], refs[groups:]
    own, other, refs = refs[:3], refs[3:6], refs[6:]
    outs, (rows_ref, done_ref, hid_ref) = refs[:groups], refs[groups:]
    n = xs[0].shape[0]

    @pl.when(flags_ref[9] == 1)
    def _():
        for g in range(groups):
            rows_ref[g * n : (g + 1) * n, :] = xs[g][...]

    @pl.when(flags_ref[8] == 1)
    def _():
        ffn_rows(rows_ref, done_ref, hid_ref, *own)

    @pl.when((flags_ref[8] == 0) & (flags_ref[9] == 1))
    def _():
        ffn_rows(rows_ref, done_ref, hid_ref, *other)

    @pl.when(flags_ref[9] == 0)
    def _():
        done_ref[...] = jnp.zeros_like(done_ref)

    for g in range(groups):
        outs[g][...] = done_ref[g * n : (g + 1) * n, :]


def hot_ffn(flags, xs, own, other):
    n, width = xs[0].shape
    inner = own[0].shape[2]
    rows = n * len(xs)
    rows_scratch, hid_scratch = ffn_scratch(rows, width, inner)
    return pl.pallas_call(
        hot_kernel,
        in_specs=[SMEM] + [VMEM] * (len(xs) + 6),
        out_specs=[VMEM] * len(xs),
        out_shape=[jax.ShapeDtypeStruct((n, width), BF16)] * len(xs),
        scratch_shapes=[rows_scratch, rows_scratch, hid_scratch],
        compiler_params=pltpu.CompilerParams(vmem_limit_bytes=44 * 2**20),
        cost_estimate=ffn_cost(rows, width, inner),
        name="hot_ffn",
    )(flags, *xs, *own, *other)


def join_kernel(flags_ref, served_ref, *refs):
    own, back = refs[:SPARE], refs[SPARE : SPARE + len(DIRS)]
    out_ref, pick_ref = refs[SPARE + len(DIRS) :]
    n, lines, _ = out_ref.shape
    width = served_ref.shape[1]
    half = width // 2
    out_ref[:, :, :width] = served_ref[...].reshape(n, lines, width)
    for s in range(SPARE):
        for d, source in enumerate((own[s],) + back):
            @pl.when(flags_ref[6 + s] == d)
            def _():
                for t in range(2):
                    at = (2 * s + t) * n
                    pick_ref[at : at + n, :] = source[:, t * half : (t + 1) * half]

    row = lax.broadcasted_iota(jnp.int32, (n * lines, lines * n), 0)
    column = lax.broadcasted_iota(jnp.int32, (n * lines, lines * n), 1)
    put = ((row & (lines - 1)) * n + row // lines == column).astype(BF16)
    placed = jnp.dot(put, pick_ref[...], preferred_element_type=F32)
    out_ref[:, :, width:] = placed.astype(BF16).reshape(n, lines, half)


def join(flags, served, own, back):
    n, width = own[0].shape
    return pl.pallas_call(
        join_kernel,
        in_specs=[SMEM] + [VMEM] * (1 + SPARE + len(DIRS)),
        out_specs=VMEM,
        out_shape=jax.ShapeDtypeStruct((n, BASE, width * CAP // BASE), BF16),
        scratch_shapes=[pltpu.VMEM((n * BASE, width // 2), BF16)],
        compiler_params=pltpu.CompilerParams(vmem_limit_bytes=32 * 2**20),
        name="join",
    )(flags, served, *own, *back)


def mix_kernel(score_ref, slot_ref, ans_ref, out_ref):
    rows, picks = slot_ref.shape
    n, lines, _ = ans_ref.shape
    width = out_ref.shape[1]
    half = width // 2
    scores = score_ref[...]
    weights = scores / jnp.sum(scores, axis=1, keepdims=True)
    slots = slot_ref[...]
    place, turn = slots >> 3, slots & 7
    base = jnp.where(turn < BASE, place * lines + turn, -2)
    spare = jnp.where(turn < BASE, -2, place * lines + 2 * (turn - BASE))

    def spread_weights(at):
        wide = lax.broadcasted_iota(jnp.int32, (rows, n * lines), 1)
        full = jnp.zeros(wide.shape, F32)
        for k in range(picks):
            full = jnp.where(at[:, k : k + 1] == wide, weights[:, k : k + 1], full)
        high = full.astype(BF16)
        low = (full - high.astype(F32)).astype(BF16)
        return jnp.concatenate([high, low], axis=0)

    base_mix = spread_weights(base)
    answers = ans_ref[:, :, :width].reshape(n * lines, width)
    extra = ans_ref[:, :, width:].reshape(n * lines, half)
    for t in range(2):
        at = slice(t * half, (t + 1) * half)
        part = jnp.dot(base_mix, answers[:, at], preferred_element_type=F32)
        part += jnp.dot(spread_weights(spare + t), extra, preferred_element_type=F32)
        out_ref[:, at] = (part[:rows] + part[rows:]).astype(BF16)


def mix(scores, slots, answers):
    n, lines, wide = answers.shape
    return pl.pallas_call(
        mix_kernel,
        in_specs=[VMEM] * 3,
        out_specs=VMEM,
        out_shape=jax.ShapeDtypeStruct((slots.shape[0], wide * BASE // CAP), BF16),
        compiler_params=pltpu.CompilerParams(vmem_limit_bytes=32 * 2**20),
        name="mix",
    )(scores, slots, answers)


def exchange(x):
    return lax.all_to_all(x, "expert", split_axis=0, concat_axis=0, tiled=True)


def relayed(scores, w_gate, w_up, w_down, base, spare, slots, meta):
    n = lax.axis_size("expert")
    flags = meta[0]
    swap = [(i, i ^ 1) for i in range(n)]
    own = (w_gate, w_up, w_down)
    other = [lax.ppermute(w, "expert", swap) for w in own]
    got_spare, base, *other = lax.optimization_barrier((exchange(spare), base, *other))
    got_base = exchange(base)
    parts = spread(flags, got_spare)
    kept, sent = parts[:SPARE], parts[SPARE:]
    hopped = [
        lax.ppermute(x, "expert", hop_pairs(axis, step, n)) for x, (axis, step) in zip(sent, DIRS)
    ]
    first = hot_ffn(flags, list(kept) + hopped[:2], own, other)
    second = hot_ffn(flags, hopped[2:], own, other)
    back = [
        lax.ppermute(x, "expert", hop_pairs(axis, -step, n))
        for x, (axis, step) in zip(list(first[SPARE:]) + list(second), DIRS)
    ]
    got_base, *_ = lax.optimization_barrier((got_base, *second))
    served = ffn(got_base, *own)
    return mix(scores, slots, exchange(join(flags, served, first[:SPARE], back)))


def expert_ffn(rows, gate_mat, up_mat, down_mat):
    gate_act = jnp.dot(rows, gate_mat, preferred_element_type=F32)
    upper = jnp.dot(rows, up_mat, preferred_element_type=F32)
    hidden = (jax.nn.silu(gate_act) * upper).astype(BF16)
    return jnp.dot(hidden, down_mat, preferred_element_type=F32).astype(BF16)


def direct(tokens, ids, scores, w_gate, w_up, w_down):
    rows, picks = ids.shape
    n = lax.axis_size("expert")
    width = tokens.shape[1]
    weights = scores / jnp.sum(scores, axis=1, keepdims=True)
    flat = ids.reshape(-1)
    experts = jnp.arange(n, dtype=jnp.int32)
    member = (flat[:, None] == experts[None, :]).astype(jnp.int32)
    before = jnp.cumsum(member, axis=0) - member
    target = flat * MOST + jnp.sum(before * member, axis=1)
    sent = jnp.zeros((n * MOST, width), BF16).at[target].set(jnp.repeat(tokens, picks, axis=0))
    got = exchange(sent.reshape(n, MOST * LINES, 128))
    served = expert_ffn(got.reshape(n * MOST, width), w_gate[0], w_up[0], w_down[0])
    answered = exchange(served.reshape(n, MOST * LINES, 128)).reshape(n * MOST, width)
    picked = weights.reshape(-1)[:, None] * answered[target].astype(F32)
    return jnp.sum(picked.reshape(rows, picks, width), axis=1).astype(BF16)


def body(tokens, ids, scores, w_gate, w_up, w_down):
    me = lax.axis_index("expert").astype(jnp.int32).reshape(1)
    base, spare, slots, meta = plan(me, ids, tokens)
    mixed = relayed(scores, w_gate, w_up, w_down, base, spare, slots, meta)
    return lax.cond(
        meta[0, 10] == 1,
        lambda mixed, *rest: mixed,
        lambda mixed, *rest: direct(*rest),
        mixed, tokens, ids, scores, w_gate, w_up, w_down,
    )


def solution(mesh):
    placed = (
        P("expert", None),
        P("expert", None),
        P("expert", None),
        P("expert", None, None),
        P("expert", None, None),
        P("expert", None, None),
    )
    return jax.shard_map(
        body, mesh=mesh, in_specs=placed, out_specs=P("expert", None), check_vma=False
    )
```

```python
import functools

import jax
import jax.numpy as jnp
from jax import lax
from jax.experimental import pallas as pl
from jax.experimental.pallas import tpu as pltpu
from jax.sharding import PartitionSpec as P

MOST = 18
BASE = 4
SPARE = 2
CAP = BASE + SPARE
HOT = 3
LINES = 16
DIRS = ((0, 1), (0, -1), (1, 1), (1, -1), (2, 1), (2, -1))
F32 = jnp.float32
BF16 = jnp.bfloat16


def split_index(i):
    return (i >> 5) & 3, (i >> 3) & 3, (i >> 1) & 3


def moved_chip(i, axis, step):
    c = list(split_index(i))
    c[axis] = (c[axis] + step) & 3
    return (c[0] * 4 + c[1]) * 4 + c[2]


def hop_pairs(axis, step, n):
    return [(i, moved_chip(i, axis, step) * 2 + (i & 1)) for i in range(n)]


def plan_kernel(me_ref, ids_ref, tok_ref, base_ref, spare_ref, slot_ref, meta_ref):
    rows, picks = ids_ref.shape
    n = 128
    me = me_ref[0]
    lane = lax.broadcasted_iota(jnp.int32, (1, n), 1)
    lower = (
        lax.broadcasted_iota(jnp.int32, (rows, rows), 1)
        < lax.broadcasted_iota(jnp.int32, (rows, rows), 0)
    ).astype(BF16)
    upper = (
        lax.broadcasted_iota(jnp.int32, (n, n), 0) < lax.broadcasted_iota(jnp.int32, (n, n), 1)
    ).astype(BF16)

    def before_lane(flags):
        wide = jnp.broadcast_to(flags, (8, n)).astype(BF16)
        return jnp.dot(wide, upper, preferred_element_type=F32)[0:1]

    ids = ids_ref[...]
    lane_rows = lax.broadcasted_iota(jnp.int32, (rows, n), 1)
    run = jnp.zeros((1, n), F32)
    ranks, members = [], []
    for k in range(picks):
        member = (ids[:, k : k + 1] == lane_rows).astype(F32)
        ahead = jnp.dot(lower, member.astype(BF16), preferred_element_type=F32) + run
        ranks.append(jnp.sum(ahead * member, axis=1, keepdims=True).astype(jnp.int32))
        members.append(member)
        run = run + jnp.sum(member, axis=0, keepdims=True)
    hot = (run > BASE + 0.5).astype(F32)
    hot_rank = before_lane(hot)

    chips, near, same = [], [], []
    dev = split_index(lane)
    for h in range(HOT):
        mine = hot * (hot_rank == float(h)).astype(F32)
        where_hot = jnp.sum(lane.astype(F32) * mine, axis=1, keepdims=True).astype(jnp.int32)
        chips.append(where_hot >> 1)
        dist = jnp.zeros((1, n), jnp.int32)
        for a, b in zip(dev, split_index(where_hot)):
            gap = (a - b) & 3
            dist = dist + jnp.minimum(gap, 4 - gap)
        same.append((dist == 0).astype(F32))
        near.append((dist == 1).astype(F32))
    taken = jnp.minimum(same[0] + same[1] + same[2], 1.0)
    near = [v * (1.0 - taken) for v in near]
    avail, slot_of, order = [], [], []
    used = jnp.zeros((1, n), F32)
    ok = jnp.ones((1, 1), F32)
    for h in range(HOT):
        free = near[h] * (used < SPARE - 0.5).astype(F32)
        avail.append(free)
        slot_of.append(used)
        order.append(before_lane(free))
        used = used + free
        enough = jnp.sum(free, axis=1, keepdims=True) > MOST - CAP - SPARE - 0.5
        ok = ok * enough.astype(F32)
    for a, b in ((0, 1), (0, 2), (1, 2)):
        ok = ok * (chips[a] != chips[b]).astype(F32)

    base_wide = lax.broadcasted_iota(jnp.int32, (rows, n * BASE), 1)
    spare_wide = lax.broadcasted_iota(jnp.int32, (rows, n * SPARE), 1)
    lane_f = lane.astype(F32)
    chosen_base = jnp.zeros(base_wide.shape, F32)
    chosen_spare = jnp.zeros(spare_wide.shape, F32)
    slot_cols = []
    for k in range(picks):
        e, q, member = ids[:, k : k + 1], ranks[k], members[k]
        which = jnp.sum(member * (hot * (hot_rank + 1.0)), axis=1, keepdims=True)
        code = jnp.where(q < CAP, e * 8 + q, (e ^ 1) * 8 + BASE + (q - CAP))
        far = jnp.zeros((rows, 1), F32)
        turn = (q - (CAP + SPARE)).astype(F32)
        for h in range(HOT):
            hit = avail[h] * (order[h] == turn).astype(F32) * (which == h + 1.0).astype(F32)
            far = far + jnp.sum(hit * (lane_f * 8 + BASE + slot_of[h]), axis=1, keepdims=True)
        code = jnp.where(q < CAP + SPARE, code, far.astype(jnp.int32))
        slot_cols.append(code)
        place, turn = code >> 3, code & 7
        at = jnp.where(turn < BASE, place * BASE + turn, -1)
        chosen_base = chosen_base + (at == base_wide).astype(F32)
        at = jnp.where(turn < BASE, -1, place * SPARE + turn - BASE)
        chosen_spare = chosen_spare + (at == spare_wide).astype(F32)
    slot_ref[...] = jnp.concatenate(slot_cols, axis=1)
    for chosen, out_ref in ((chosen_spare, spare_ref), (chosen_base, base_ref)):
        picked = lax.dot_general(
            chosen.astype(BF16), tok_ref[...], (((0,), (0,)), ((), ())),
            preferred_element_type=F32,
        )
        out_ref[...] = picked.astype(BF16).reshape(out_ref.shape)

    here = (lane == me).astype(F32)
    meta = jnp.zeros((1, n), F32)
    source = [jnp.zeros((1, n), F32) for _ in range(SPARE)]
    for d, (axis, step) in enumerate(DIRS):
        target = moved_chip(lane, axis, step)
        sent = jnp.zeros((1, n), F32)
        for h in range(HOT):
            serves = avail[h] * (target == chips[h]).astype(F32)
            sent = sent + serves * slot_of[h]
            for j in range(SPARE):
                source[j] = source[j] + serves * (slot_of[h] == float(j)).astype(F32) * (1.0 + d)
        meta = jnp.where(lane == d, jnp.sum(sent * here, axis=1, keepdims=True), meta)
    for j in range(SPARE):
        meta = jnp.where(lane == 6 + j, jnp.sum(source[j] * here, axis=1, keepdims=True), meta)
    meta = jnp.where(lane == 8, jnp.sum(hot * here, axis=1, keepdims=True), meta)
    meta = jnp.where(lane == 9, jnp.sum(taken * here, axis=1, keepdims=True), meta)
    meta = jnp.where(lane == 10, ok, meta)
    meta_ref[...] = meta.astype(jnp.int32)


def plan(me, ids, tokens):
    rows, width = tokens.shape
    vmem = pl.BlockSpec(memory_space=pltpu.VMEM)
    return pl.pallas_call(
        plan_kernel,
        in_specs=[pl.BlockSpec(memory_space=pltpu.SMEM), vmem, vmem],
        out_specs=[vmem] * 4,
        out_shape=[
            jax.ShapeDtypeStruct((128, BASE, width), BF16),
            jax.ShapeDtypeStruct((128, SPARE, width), BF16),
            jax.ShapeDtypeStruct(ids.shape, jnp.int32),
            jax.ShapeDtypeStruct((1, 128), jnp.int32),
        ],
        compiler_params=pltpu.CompilerParams(vmem_limit_bytes=60 * 2**20),
        name="plan",
    )(me, ids, tokens)


VMEM = pl.BlockSpec(memory_space=pltpu.VMEM)
SMEM = pl.BlockSpec(memory_space=pltpu.SMEM)
HBM = pl.BlockSpec(memory_space=pltpu.HBM)
BLOCK = 256


def spread_kernel(flags_ref, got_ref, *refs):
    outs, parts_ref, sems = refs[:-2], refs[-2], refs[-1]
    n, spare, width = got_ref.shape
    got = got_ref[...].reshape(n * spare, width)
    row = lax.broadcasted_iota(jnp.int32, (n, n * spare), 0)
    column = lax.broadcasted_iota(jnp.int32, (n, n * spare), 1)
    for s in range(SPARE):
        take = (row * spare + s == column).astype(BF16)
        parts_ref[s] = jnp.dot(take, got, preferred_element_type=F32).astype(BF16)
    copies = [
        pltpu.make_async_copy(parts_ref.at[i if i < SPARE else flags_ref[i - SPARE]], out, sems.at[i])
        for i, out in enumerate(outs)
    ]
    for copy in copies:
        copy.start()
    for copy in copies:
        copy.wait()


def spread(flags, got):
    n, spare, width = got.shape
    count = SPARE + len(DIRS)
    return pl.pallas_call(
        spread_kernel,
        in_specs=[SMEM, VMEM],
        out_specs=[HBM] * count,
        out_shape=[jax.ShapeDtypeStruct((n, width), BF16)] * count,
        scratch_shapes=[pltpu.VMEM((SPARE, n, width), BF16), pltpu.SemaphoreType.DMA((count,))],
        compiler_params=pltpu.CompilerParams(vmem_limit_bytes=60 * 2**20),
        name="spread",
    )(flags, got)


HALVES = 2


def ffn_rows(x_ref, out_ref, weights, scratch, arriving=()):
    gate, up, down = weights
    hid_ref, gate_ref, up_ref, down_ref, sems = scratch
    blocks = hid_ref.shape[0]
    width = x_ref.shape[1]
    half = width // HALVES
    copies = []
    for p in range(blocks):
        at = pl.ds(p * BLOCK, BLOCK)
        copies.append(pltpu.make_async_copy(gate.at[0, :, at], gate_ref.at[p], sems.at[2 * p]))
        copies.append(pltpu.make_async_copy(up.at[0, :, at], up_ref.at[p], sems.at[2 * p + 1]))
    for c in range(HALVES):
        at = pl.ds(c * half, half)
        copies.append(
            pltpu.make_async_copy(down.at[0, :, at], down_ref.at[c], sems.at[2 * blocks + c])
        )
    for copy in copies:
        copy.start()
    for copy in arriving:
        copy.wait()
    for p in range(blocks):
        copies[2 * p].wait()
        copies[2 * p + 1].wait()
        x = x_ref[...]
        gate_act = jnp.dot(x, gate_ref[p], preferred_element_type=F32)
        upper = jnp.dot(x, up_ref[p], preferred_element_type=F32)
        hid_ref[p] = (jax.nn.silu(gate_act) * upper).astype(BF16)
    for c in range(HALVES):
        copies[2 * blocks + c].wait()
        for at in range(0, half, 512):
            part = jnp.dot(
                hid_ref[0], down_ref[c, :BLOCK, at : at + 512], preferred_element_type=F32
            )
            for p in range(1, blocks):
                part += jnp.dot(
                    hid_ref[p], down_ref[c, p * BLOCK : (p + 1) * BLOCK, at : at + 512],
                    preferred_element_type=F32,
                )
            out_ref[:, c * half + at : c * half + at + 512] = part.astype(BF16)


def ffn_scratch(rows, width, inner, more=0):
    blocks = inner // BLOCK
    return [
        pltpu.VMEM((blocks, rows, BLOCK), BF16),
        pltpu.VMEM((blocks, width, BLOCK), BF16),
        pltpu.VMEM((blocks, width, BLOCK), BF16),
        pltpu.VMEM((HALVES, inner, width // HALVES), BF16),
        pltpu.SemaphoreType.DMA((2 * blocks + HALVES + more,)),
    ]


def ffn_cost(rows, width, inner):
    return pl.CostEstimate(
        flops=6 * rows * width * inner, bytes_accessed=6 * width * inner, transcendentals=0
    )


def ffn_kernel(x_ref, gate, up, down, out_ref, rows_ref, *scratch):
    rows_ref[...] = x_ref[...].reshape(rows_ref.shape)
    ffn_rows(rows_ref, out_ref, (gate, up, down), scratch)


def ffn(x, gate_mat, up_mat, down_mat):
    n, slots, width = x.shape
    inner = gate_mat.shape[2]
    rows = n * slots
    return pl.pallas_call(
        ffn_kernel,
        in_specs=[VMEM] + [HBM] * 3,
        out_specs=VMEM,
        out_shape=jax.ShapeDtypeStruct((rows, width), BF16),
        scratch_shapes=[pltpu.VMEM((rows, width), BF16)] + ffn_scratch(rows, width, inner),
        compiler_params=pltpu.CompilerParams(vmem_limit_bytes=60 * 2**20),
        cost_estimate=ffn_cost(rows, width, inner),
        name="ffn",
    )(x, gate_mat, up_mat, down_mat)


def hot_kernel(groups, flags_ref, *refs):
    xs, refs = refs[:groups], refs[groups:]
    own, other, refs = refs[:3], refs[3:6], refs[6:]
    outs, (rows_ref, done_ref, *scratch) = refs[:groups], refs[groups:]
    n = xs[0].shape[0]
    sems = scratch[-1]
    base = sems.shape[0] - groups

    def work(weights):
        parts = [pl.ds(g * n, n) for g in range(groups)]
        arriving = [
            pltpu.make_async_copy(x, rows_ref.at[at], sems.at[base + g])
            for g, (x, at) in enumerate(zip(xs, parts))
        ]
        for copy in arriving:
            copy.start()
        ffn_rows(rows_ref, done_ref, weights, scratch, arriving)
        leaving = [
            pltpu.make_async_copy(done_ref.at[at], out, sems.at[base + g])
            for g, (out, at) in enumerate(zip(outs, parts))
        ]
        for copy in leaving:
            copy.start()
        for copy in leaving:
            copy.wait()

    @pl.when(flags_ref[8] == 1)
    def _():
        work(own)

    @pl.when((flags_ref[8] == 0) & (flags_ref[9] == 1))
    def _():
        work(other)


def hot_ffn(flags, xs, own, other):
    n, width = xs[0].shape
    inner = own[0].shape[2]
    rows = n * len(xs)
    return pl.pallas_call(
        functools.partial(hot_kernel, len(xs)),
        in_specs=[SMEM] + [HBM] * (len(xs) + 6),
        out_specs=[HBM] * len(xs),
        out_shape=[jax.ShapeDtypeStruct((n, width), BF16)] * len(xs),
        scratch_shapes=[pltpu.VMEM((rows, width), BF16)] * 2
        + ffn_scratch(rows, width, inner, len(xs)),
        compiler_params=pltpu.CompilerParams(vmem_limit_bytes=60 * 2**20),
        cost_estimate=ffn_cost(rows, width, inner),
        name="hot_ffn",
    )(flags, *xs, *own, *other)


def join_kernel(flags_ref, served_ref, *refs):
    own, back = refs[:SPARE], refs[SPARE : SPARE + len(DIRS)]
    out_ref, pick_ref, sems = refs[SPARE + len(DIRS) :]
    n, lines, _ = out_ref.shape
    width = served_ref.shape[1]
    half = width // 2
    for s in range(SPARE):
        at = pl.ds(2 * s * n, 2 * n)

        @pl.when((flags_ref[6 + s] == 0) & (flags_ref[9] == 0))
        def _():
            pick_ref[at, :] = jnp.zeros((2 * n, half), BF16)

        for d, source in enumerate((own[s],) + back):
            @pl.when((flags_ref[6 + s] == d) & ((d > 0) | (flags_ref[9] == 1)))
            def _():
                copies = [
                    pltpu.make_async_copy(
                        source.at[:, pl.ds(t * half, half)],
                        pick_ref.at[pl.ds((2 * s + t) * n, n)],
                        sems.at[t],
                    )
                    for t in range(2)
                ]
                for copy in copies:
                    copy.start()
                for copy in copies:
                    copy.wait()

    out_ref[:, :, :width] = served_ref[...].reshape(n, lines, width)
    row = lax.broadcasted_iota(jnp.int32, (n * lines, lines * n), 0)
    column = lax.broadcasted_iota(jnp.int32, (n * lines, lines * n), 1)
    put = ((row & (lines - 1)) * n + row // lines == column).astype(BF16)
    placed = jnp.dot(put, pick_ref[...], preferred_element_type=F32)
    out_ref[:, :, width:] = placed.astype(BF16).reshape(n, lines, half)


def join(flags, served, own, back):
    n, width = own[0].shape
    return pl.pallas_call(
        join_kernel,
        in_specs=[SMEM, VMEM] + [HBM] * (SPARE + len(DIRS)),
        out_specs=VMEM,
        out_shape=jax.ShapeDtypeStruct((n, BASE, width * CAP // BASE), BF16),
        scratch_shapes=[pltpu.VMEM((n * BASE, width // 2), BF16), pltpu.SemaphoreType.DMA((2,))],
        compiler_params=pltpu.CompilerParams(vmem_limit_bytes=60 * 2**20),
        name="join",
    )(flags, served, *own, *back)


def mix_kernel(score_ref, slot_ref, ans_ref, out_ref):
    rows, picks = slot_ref.shape
    n, lines, _ = ans_ref.shape
    width = out_ref.shape[1]
    half = width // 2
    scores = score_ref[...]
    weights = scores / jnp.sum(scores, axis=1, keepdims=True)
    slots = slot_ref[...]
    place, turn = slots >> 3, slots & 7
    base = jnp.where(turn < BASE, place * lines + turn, -2)
    spare = jnp.where(turn < BASE, -2, place * lines + 2 * (turn - BASE))

    def spread_weights(at):
        wide = lax.broadcasted_iota(jnp.int32, (rows, n * lines), 1)
        full = jnp.zeros(wide.shape, F32)
        for k in range(picks):
            full = jnp.where(at[:, k : k + 1] == wide, weights[:, k : k + 1], full)
        high = full.astype(BF16)
        low = (full - high.astype(F32)).astype(BF16)
        return jnp.concatenate([high, low], axis=0)

    base_mix = spread_weights(base)
    answers = ans_ref[:, :, :width].reshape(n * lines, width)
    extra = ans_ref[:, :, width:].reshape(n * lines, half)
    for t in range(2):
        at = slice(t * half, (t + 1) * half)
        part = jnp.dot(base_mix, answers[:, at], preferred_element_type=F32)
        part += jnp.dot(spread_weights(spare + t), extra, preferred_element_type=F32)
        out_ref[:, at] = (part[:rows] + part[rows:]).astype(BF16)


def mix(scores, slots, answers):
    n, lines, wide = answers.shape
    return pl.pallas_call(
        mix_kernel,
        in_specs=[VMEM] * 3,
        out_specs=VMEM,
        out_shape=jax.ShapeDtypeStruct((slots.shape[0], wide * BASE // CAP), BF16),
        compiler_params=pltpu.CompilerParams(vmem_limit_bytes=60 * 2**20),
        name="mix",
    )(scores, slots, answers)


def exchange(x):
    return lax.all_to_all(x, "expert", split_axis=0, concat_axis=0, tiled=True)


def relayed(scores, w_gate, w_up, w_down, base, spare, slots, meta):
    n = lax.axis_size("expert")
    flags = meta[0]
    swap = [(i, i ^ 1) for i in range(n)]
    own = (w_gate, w_up, w_down)
    other = [lax.ppermute(w, "expert", swap) for w in own]
    got_spare, *other = lax.optimization_barrier((exchange(spare), *other))
    parts = spread(flags, got_spare)
    kept, sent = parts[:SPARE], parts[SPARE:]
    hopped = [
        lax.ppermute(x, "expert", hop_pairs(axis, step, n)) for x, (axis, step) in zip(sent, DIRS)
    ]
    first = hot_ffn(flags, kept, own, other)
    base, first, hopped = lax.optimization_barrier((base, first, hopped))
    got_base = exchange(base)
    second = hot_ffn(flags, hopped[:3], own, other)
    third = hot_ffn(flags, hopped[3:], own, other)
    back = [
        lax.ppermute(x, "expert", hop_pairs(axis, -step, n))
        for x, (axis, step) in zip(list(second) + list(third), DIRS)
    ]
    got_base, *_ = lax.optimization_barrier((got_base, *third))
    served = ffn(got_base, *own)
    return mix(scores, slots, exchange(join(flags, served, first, back)))


def expert_ffn(rows, gate_mat, up_mat, down_mat):
    gate_act = jnp.dot(rows, gate_mat, preferred_element_type=F32)
    upper = jnp.dot(rows, up_mat, preferred_element_type=F32)
    hidden = (jax.nn.silu(gate_act) * upper).astype(BF16)
    return jnp.dot(hidden, down_mat, preferred_element_type=F32).astype(BF16)


def direct(tokens, ids, scores, w_gate, w_up, w_down):
    rows, picks = ids.shape
    n = lax.axis_size("expert")
    width = tokens.shape[1]
    weights = scores / jnp.sum(scores, axis=1, keepdims=True)
    flat = ids.reshape(-1)
    experts = jnp.arange(n, dtype=jnp.int32)
    member = (flat[:, None] == experts[None, :]).astype(jnp.int32)
    before = jnp.cumsum(member, axis=0) - member
    target = flat * MOST + jnp.sum(before * member, axis=1)
    sent = jnp.zeros((n * MOST, width), BF16).at[target].set(jnp.repeat(tokens, picks, axis=0))
    got = exchange(sent.reshape(n, MOST * LINES, 128))
    served = expert_ffn(got.reshape(n * MOST, width), w_gate[0], w_up[0], w_down[0])
    answered = exchange(served.reshape(n, MOST * LINES, 128)).reshape(n * MOST, width)
    picked = weights.reshape(-1)[:, None] * answered[target].astype(F32)
    return jnp.sum(picked.reshape(rows, picks, width), axis=1).astype(BF16)


def body(tokens, ids, scores, w_gate, w_up, w_down):
    me = lax.axis_index("expert").astype(jnp.int32).reshape(1)
    base, spare, slots, meta = plan(me, ids, tokens)
    mixed = relayed(scores, w_gate, w_up, w_down, base, spare, slots, meta)
    return lax.cond(
        meta[0, 10] == 1,
        lambda mixed, *rest: mixed,
        lambda mixed, *rest: direct(*rest),
        mixed, tokens, ids, scores, w_gate, w_up, w_down,
    )


def solution(mesh):
    placed = (
        P("expert", None),
        P("expert", None),
        P("expert", None),
        P("expert", None, None),
        P("expert", None, None),
        P("expert", None, None),
    )
    return jax.shard_map(
        body, mesh=mesh, in_specs=placed, out_specs=P("expert", None), check_vma=False
    )
```

```python
import functools

import jax
import jax.numpy as jnp
from jax import lax
from jax.experimental import pallas as pl
from jax.experimental.pallas import tpu as pltpu
from jax.sharding import PartitionSpec as P

MOST = 18
BASE = 4
SPARE = 2
CAP = BASE + SPARE
HOT = 3
LINES = 16
DIRS = ((0, 1), (0, -1), (1, 1), (1, -1), (2, 1), (2, -1))
F32 = jnp.float32
BF16 = jnp.bfloat16


def split_index(i):
    return (i >> 5) & 3, (i >> 3) & 3, (i >> 1) & 3


def moved_chip(i, axis, step):
    c = list(split_index(i))
    c[axis] = (c[axis] + step) & 3
    return (c[0] * 4 + c[1]) * 4 + c[2]


def hop_pairs(axis, step, n):
    return [(i, moved_chip(i, axis, step) * 2 + (i & 1)) for i in range(n)]


def plan_kernel(me_ref, ids_ref, tok_ref, base_ref, spare_ref, slot_ref, meta_ref):
    rows, picks = ids_ref.shape
    n = 128
    me = me_ref[0]
    lane = lax.broadcasted_iota(jnp.int32, (1, n), 1)
    lower = (
        lax.broadcasted_iota(jnp.int32, (rows, rows), 1)
        < lax.broadcasted_iota(jnp.int32, (rows, rows), 0)
    ).astype(BF16)
    upper = (
        lax.broadcasted_iota(jnp.int32, (n, n), 0) < lax.broadcasted_iota(jnp.int32, (n, n), 1)
    ).astype(BF16)

    def before_lane(flags):
        wide = jnp.broadcast_to(flags, (8, n)).astype(BF16)
        return jnp.dot(wide, upper, preferred_element_type=F32)[0:1]

    ids = ids_ref[...]
    lane_rows = lax.broadcasted_iota(jnp.int32, (rows, n), 1)
    run = jnp.zeros((1, n), F32)
    ranks, members = [], []
    for k in range(picks):
        member = (ids[:, k : k + 1] == lane_rows).astype(F32)
        ahead = jnp.dot(lower, member.astype(BF16), preferred_element_type=F32) + run
        ranks.append(jnp.sum(ahead * member, axis=1, keepdims=True).astype(jnp.int32))
        members.append(member)
        run = run + jnp.sum(member, axis=0, keepdims=True)
    hot = (run > BASE + 0.5).astype(F32)
    hot_rank = before_lane(hot)

    chips, near, same = [], [], []
    dev = split_index(lane)
    for h in range(HOT):
        mine = hot * (hot_rank == float(h)).astype(F32)
        where_hot = jnp.sum(lane.astype(F32) * mine, axis=1, keepdims=True).astype(jnp.int32)
        chips.append(where_hot >> 1)
        dist = jnp.zeros((1, n), jnp.int32)
        for a, b in zip(dev, split_index(where_hot)):
            gap = (a - b) & 3
            dist = dist + jnp.minimum(gap, 4 - gap)
        same.append((dist == 0).astype(F32))
        near.append((dist == 1).astype(F32))
    taken = jnp.minimum(same[0] + same[1] + same[2], 1.0)
    near = [v * (1.0 - taken) for v in near]
    avail, slot_of, order = [], [], []
    used = jnp.zeros((1, n), F32)
    ok = jnp.ones((1, 1), F32)
    for h in range(HOT):
        free = near[h] * (used < SPARE - 0.5).astype(F32)
        avail.append(free)
        slot_of.append(used)
        order.append(before_lane(free))
        used = used + free
        enough = jnp.sum(free, axis=1, keepdims=True) > MOST - CAP - SPARE - 0.5
        ok = ok * enough.astype(F32)
    for a, b in ((0, 1), (0, 2), (1, 2)):
        ok = ok * (chips[a] != chips[b]).astype(F32)

    base_wide = lax.broadcasted_iota(jnp.int32, (rows, n * BASE), 1)
    spare_wide = lax.broadcasted_iota(jnp.int32, (rows, n * SPARE), 1)
    lane_f = lane.astype(F32)
    chosen_base = jnp.zeros(base_wide.shape, F32)
    chosen_spare = jnp.zeros(spare_wide.shape, F32)
    slot_cols = []
    for k in range(picks):
        e, q, member = ids[:, k : k + 1], ranks[k], members[k]
        which = jnp.sum(member * (hot * (hot_rank + 1.0)), axis=1, keepdims=True)
        code = jnp.where(q < CAP, e * 8 + q, (e ^ 1) * 8 + BASE + (q - CAP))
        far = jnp.zeros((rows, 1), F32)
        turn = (q - (CAP + SPARE)).astype(F32)
        for h in range(HOT):
            hit = avail[h] * (order[h] == turn).astype(F32) * (which == h + 1.0).astype(F32)
            far = far + jnp.sum(hit * (lane_f * 8 + BASE + slot_of[h]), axis=1, keepdims=True)
        code = jnp.where(q < CAP + SPARE, code, far.astype(jnp.int32))
        slot_cols.append(code)
        place, turn = code >> 3, code & 7
        at = jnp.where(turn < BASE, place * BASE + turn, -1)
        chosen_base = chosen_base + (at == base_wide).astype(F32)
        at = jnp.where(turn < BASE, -1, place * SPARE + turn - BASE)
        chosen_spare = chosen_spare + (at == spare_wide).astype(F32)
    slot_ref[...] = jnp.concatenate(slot_cols, axis=1)
    for chosen, out_ref in ((chosen_spare, spare_ref), (chosen_base, base_ref)):
        picked = lax.dot_general(
            chosen.astype(BF16), tok_ref[...], (((0,), (0,)), ((), ())),
            preferred_element_type=F32,
        )
        out_ref[...] = picked.astype(BF16).reshape(out_ref.shape)

    here = (lane == me).astype(F32)
    meta = jnp.zeros((1, n), F32)
    source = [jnp.zeros((1, n), F32) for _ in range(SPARE)]
    for d, (axis, step) in enumerate(DIRS):
        target = moved_chip(lane, axis, step)
        sent = jnp.zeros((1, n), F32)
        for h in range(HOT):
            serves = avail[h] * (target == chips[h]).astype(F32)
            sent = sent + serves * slot_of[h]
            for j in range(SPARE):
                source[j] = source[j] + serves * (slot_of[h] == float(j)).astype(F32) * (1.0 + d)
        meta = jnp.where(lane == d, jnp.sum(sent * here, axis=1, keepdims=True), meta)
    for j in range(SPARE):
        meta = jnp.where(lane == 6 + j, jnp.sum(source[j] * here, axis=1, keepdims=True), meta)
    meta = jnp.where(lane == 8, jnp.sum(hot * here, axis=1, keepdims=True), meta)
    meta = jnp.where(lane == 9, jnp.sum(taken * here, axis=1, keepdims=True), meta)
    meta = jnp.where(lane == 10, ok, meta)
    meta_ref[...] = meta.astype(jnp.int32)


def plan(me, ids, tokens):
    rows, width = tokens.shape
    vmem = pl.BlockSpec(memory_space=pltpu.VMEM)
    return pl.pallas_call(
        plan_kernel,
        in_specs=[pl.BlockSpec(memory_space=pltpu.SMEM), vmem, vmem],
        out_specs=[vmem] * 4,
        out_shape=[
            jax.ShapeDtypeStruct((128, BASE, width), BF16),
            jax.ShapeDtypeStruct((128, SPARE, width), BF16),
            jax.ShapeDtypeStruct(ids.shape, jnp.int32),
            jax.ShapeDtypeStruct((1, 128), jnp.int32),
        ],
        compiler_params=pltpu.CompilerParams(vmem_limit_bytes=24 * 2**20),
        name="plan",
    )(me, ids, tokens)


VMEM = pl.BlockSpec(memory_space=pltpu.VMEM)
SMEM = pl.BlockSpec(memory_space=pltpu.SMEM)
HBM = pl.BlockSpec(memory_space=pltpu.HBM)
BLOCK = 256


def spread_kernel(flags_ref, got_ref, *refs):
    outs, parts_ref, sems = refs[:-2], refs[-2], refs[-1]
    n, spare, width = got_ref.shape
    got = got_ref[...].reshape(n * spare, width)
    row = lax.broadcasted_iota(jnp.int32, (n, n * spare), 0)
    column = lax.broadcasted_iota(jnp.int32, (n, n * spare), 1)
    for s in range(SPARE):
        take = (row * spare + s == column).astype(BF16)
        parts_ref[s] = jnp.dot(take, got, preferred_element_type=F32).astype(BF16)
    copies = [
        pltpu.make_async_copy(parts_ref.at[i if i < SPARE else flags_ref[i - SPARE]], out, sems.at[i])
        for i, out in enumerate(outs)
    ]
    for copy in copies:
        copy.start()
    for copy in copies:
        copy.wait()


def spread(flags, got):
    n, spare, width = got.shape
    count = SPARE + len(DIRS)
    return pl.pallas_call(
        spread_kernel,
        in_specs=[SMEM, VMEM],
        out_specs=[HBM] * count,
        out_shape=[jax.ShapeDtypeStruct((n, width), BF16)] * count,
        scratch_shapes=[pltpu.VMEM((SPARE, n, width), BF16), pltpu.SemaphoreType.DMA((count,))],
        compiler_params=pltpu.CompilerParams(vmem_limit_bytes=24 * 2**20),
        name="spread",
    )(flags, got)


PANEL = 512


def fetch(weights, scratch):
    gate, up, down = weights
    hid_ref, gate_ref, up_ref, down_ref, sems = scratch
    blocks, panels = gate_ref.shape[0], down_ref.shape[0]
    for p in range(blocks):
        at = pl.ds(p * BLOCK, BLOCK)
        pltpu.make_async_copy(gate.at[0, :, at], gate_ref.at[p], sems.at[2 * p]).start()
        pltpu.make_async_copy(up.at[0, :, at], up_ref.at[p], sems.at[2 * p + 1]).start()
    for c in range(panels):
        at = pl.ds(c * PANEL, PANEL)
        pltpu.make_async_copy(down.at[0, :, at], down_ref.at[c], sems.at[2 * blocks + c]).start()


def ffn_rows(x_ref, out_ref, scratch):
    hid_ref, gate_ref, up_ref, down_ref, sems = scratch
    blocks, panels = gate_ref.shape[0], down_ref.shape[0]

    @pl.loop(0, blocks)
    def _(p):
        pltpu.make_async_copy(gate_ref.at[p], gate_ref.at[p], sems.at[2 * p]).wait()
        pltpu.make_async_copy(up_ref.at[p], up_ref.at[p], sems.at[2 * p + 1]).wait()
        x = x_ref[...]
        gate_act = jnp.dot(x, gate_ref[p], preferred_element_type=F32)
        upper = jnp.dot(x, up_ref[p], preferred_element_type=F32)
        hid_ref[p] = (jax.nn.silu(gate_act) * upper).astype(BF16)

    @pl.loop(0, panels)
    def _(c):
        pltpu.make_async_copy(down_ref.at[c], down_ref.at[c], sems.at[2 * blocks + c]).wait()
        part = jnp.dot(hid_ref[0], down_ref[c, :BLOCK], preferred_element_type=F32)
        for p in range(1, blocks):
            part += jnp.dot(
                hid_ref[p], down_ref[c, p * BLOCK : (p + 1) * BLOCK], preferred_element_type=F32
            )
        out_ref[:, pl.ds(pl.multiple_of(c * PANEL, PANEL), PANEL)] = part.astype(BF16)


def ffn_scratch(rows, width, inner, more=0):
    blocks, panels = inner // BLOCK, width // PANEL
    return [
        pltpu.VMEM((blocks, rows, BLOCK), BF16),
        pltpu.VMEM((blocks, width, BLOCK), BF16),
        pltpu.VMEM((blocks, width, BLOCK), BF16),
        pltpu.VMEM((panels, inner, PANEL), BF16),
        pltpu.SemaphoreType.DMA((2 * blocks + panels + more,)),
    ]


def ffn_cost(rows, width, inner):
    return pl.CostEstimate(
        flops=6 * rows * width * inner, bytes_accessed=6 * width * inner, transcendentals=0
    )


def ffn_kernel(x_ref, gate, up, down, out_ref, rows_ref, *scratch):
    fetch((gate, up, down), scratch)
    rows_ref[...] = x_ref[...].reshape(rows_ref.shape)
    ffn_rows(rows_ref, out_ref, scratch)


def ffn(x, gate_mat, up_mat, down_mat):
    n, slots, width = x.shape
    inner = gate_mat.shape[2]
    rows = n * slots
    return pl.pallas_call(
        ffn_kernel,
        in_specs=[VMEM] + [HBM] * 3,
        out_specs=VMEM,
        out_shape=jax.ShapeDtypeStruct((rows, width), BF16),
        scratch_shapes=[pltpu.VMEM((rows, width), BF16)] + ffn_scratch(rows, width, inner),
        compiler_params=pltpu.CompilerParams(vmem_limit_bytes=40 * 2**20),
        cost_estimate=ffn_cost(rows, width, inner),
        name="ffn",
    )(x, gate_mat, up_mat, down_mat)


def hot_kernel(groups, flags_ref, *refs):
    xs, refs = refs[:groups], refs[groups:]
    own, other, refs = refs[:3], refs[3:6], refs[6:]
    outs, (rows_ref, done_ref, *scratch) = refs[:groups], refs[groups:]
    n = xs[0].shape[0]
    sems = scratch[-1]
    base = sems.shape[0] - groups

    @pl.when(flags_ref[9] == 1)
    def _():
        parts = [pl.ds(g * n, n) for g in range(groups)]
        arriving = [
            pltpu.make_async_copy(x, rows_ref.at[at], sems.at[base + g])
            for g, (x, at) in enumerate(zip(xs, parts))
        ]
        for copy in arriving:
            copy.start()

        @pl.when(flags_ref[8] == 1)
        def _():
            fetch(own, scratch)

        @pl.when(flags_ref[8] == 0)
        def _():
            fetch(other, scratch)

        for copy in arriving:
            copy.wait()
        ffn_rows(rows_ref, done_ref, scratch)
        leaving = [
            pltpu.make_async_copy(done_ref.at[at], out, sems.at[base + g])
            for g, (out, at) in enumerate(zip(outs, parts))
        ]
        for copy in leaving:
            copy.start()
        for copy in leaving:
            copy.wait()


def hot_ffn(flags, xs, own, other):
    n, width = xs[0].shape
    inner = own[0].shape[2]
    rows = n * len(xs)
    return pl.pallas_call(
        functools.partial(hot_kernel, len(xs)),
        in_specs=[SMEM] + [HBM] * (len(xs) + 6),
        out_specs=[HBM] * len(xs),
        out_shape=[jax.ShapeDtypeStruct((n, width), BF16)] * len(xs),
        scratch_shapes=[pltpu.VMEM((rows, width), BF16)] * 2
        + ffn_scratch(rows, width, inner, len(xs)),
        compiler_params=pltpu.CompilerParams(vmem_limit_bytes=60 * 2**20),
        cost_estimate=ffn_cost(rows, width, inner),
        name="hot_ffn",
    )(flags, *xs, *own, *other)


def join_kernel(flags_ref, served_ref, *refs):
    own, back = refs[:SPARE], refs[SPARE : SPARE + len(DIRS)]
    out_ref, pick_ref, sems = refs[SPARE + len(DIRS) :]
    n, lines, _ = out_ref.shape
    width = served_ref.shape[1]
    half = width // 2
    for s in range(SPARE):
        at = pl.ds(2 * s * n, 2 * n)

        @pl.when((flags_ref[6 + s] == 0) & (flags_ref[9] == 0))
        def _():
            pick_ref[at, :] = jnp.zeros((2 * n, half), BF16)

        for d, source in enumerate((own[s],) + back):
            @pl.when((flags_ref[6 + s] == d) & ((d > 0) | (flags_ref[9] == 1)))
            def _():
                copies = [
                    pltpu.make_async_copy(
                        source.at[:, pl.ds(t * half, half)],
                        pick_ref.at[pl.ds((2 * s + t) * n, n)],
                        sems.at[t],
                    )
                    for t in range(2)
                ]
                for copy in copies:
                    copy.start()
                for copy in copies:
                    copy.wait()

    out_ref[:, :, :width] = served_ref[...].reshape(n, lines, width)
    row = lax.broadcasted_iota(jnp.int32, (n * lines, lines * n), 0)
    column = lax.broadcasted_iota(jnp.int32, (n * lines, lines * n), 1)
    put = ((row & (lines - 1)) * n + row // lines == column).astype(BF16)
    placed = jnp.dot(put, pick_ref[...], preferred_element_type=F32)
    out_ref[:, :, width:] = placed.astype(BF16).reshape(n, lines, half)


def join(flags, served, own, back):
    n, width = own[0].shape
    return pl.pallas_call(
        join_kernel,
        in_specs=[SMEM, VMEM] + [HBM] * (SPARE + len(DIRS)),
        out_specs=VMEM,
        out_shape=jax.ShapeDtypeStruct((n, BASE, width * CAP // BASE), BF16),
        scratch_shapes=[pltpu.VMEM((n * BASE, width // 2), BF16), pltpu.SemaphoreType.DMA((2,))],
        compiler_params=pltpu.CompilerParams(vmem_limit_bytes=24 * 2**20),
        name="join",
    )(flags, served, *own, *back)


def mix_kernel(score_ref, slot_ref, ans_ref, out_ref):
    rows, picks = slot_ref.shape
    n, lines, _ = ans_ref.shape
    width = out_ref.shape[1]
    half = width // 2
    scores = score_ref[...]
    weights = scores / jnp.sum(scores, axis=1, keepdims=True)
    slots = slot_ref[...]
    place, turn = slots >> 3, slots & 7
    base = jnp.where(turn < BASE, place * lines + turn, -2)
    spare = jnp.where(turn < BASE, -2, place * lines + 2 * (turn - BASE))

    def spread_weights(at):
        wide = lax.broadcasted_iota(jnp.int32, (rows, n * lines), 1)
        full = jnp.zeros(wide.shape, F32)
        for k in range(picks):
            full = jnp.where(at[:, k : k + 1] == wide, weights[:, k : k + 1], full)
        high = full.astype(BF16)
        low = (full - high.astype(F32)).astype(BF16)
        return jnp.concatenate([high, low], axis=0)

    base_mix = spread_weights(base)
    answers = ans_ref[:, :, :width].reshape(n * lines, width)
    extra = ans_ref[:, :, width:].reshape(n * lines, half)
    for t in range(2):
        at = slice(t * half, (t + 1) * half)
        part = jnp.dot(base_mix, answers[:, at], preferred_element_type=F32)
        part += jnp.dot(spread_weights(spare + t), extra, preferred_element_type=F32)
        out_ref[:, at] = (part[:rows] + part[rows:]).astype(BF16)


def mix(scores, slots, answers):
    n, lines, wide = answers.shape
    return pl.pallas_call(
        mix_kernel,
        in_specs=[VMEM] * 3,
        out_specs=VMEM,
        out_shape=jax.ShapeDtypeStruct((slots.shape[0], wide * BASE // CAP), BF16),
        compiler_params=pltpu.CompilerParams(vmem_limit_bytes=24 * 2**20),
        name="mix",
    )(scores, slots, answers)


def exchange(x):
    return lax.all_to_all(x, "expert", split_axis=0, concat_axis=0, tiled=True)


def relayed(scores, w_gate, w_up, w_down, base, spare, slots, meta):
    n = lax.axis_size("expert")
    flags = meta[0]
    swap = [(i, i ^ 1) for i in range(n)]
    own = (w_gate, w_up, w_down)
    other = [lax.ppermute(w, "expert", swap) for w in own]
    got_spare, base, *other = lax.optimization_barrier((exchange(spare), base, *other))
    got_base = exchange(base)
    parts = spread(flags, got_spare)
    kept, sent = parts[:SPARE], parts[SPARE:]
    hopped = [
        lax.ppermute(x, "expert", hop_pairs(axis, step, n)) for x, (axis, step) in zip(sent, DIRS)
    ]
    first = hot_ffn(flags, kept, own, other)
    first, early = lax.optimization_barrier((first, hopped[:3]))
    second = hot_ffn(flags, early, own, other)
    third = hot_ffn(flags, hopped[3:], own, other)
    back = [
        lax.ppermute(x, "expert", hop_pairs(axis, -step, n))
        for x, (axis, step) in zip(list(second) + list(third), DIRS)
    ]
    got_base, *_ = lax.optimization_barrier((got_base, *third))
    served = ffn(got_base, *own)
    return mix(scores, slots, exchange(join(flags, served, first, back)))


def expert_ffn(rows, gate_mat, up_mat, down_mat):
    gate_act = jnp.dot(rows, gate_mat, preferred_element_type=F32)
    upper = jnp.dot(rows, up_mat, preferred_element_type=F32)
    hidden = (jax.nn.silu(gate_act) * upper).astype(BF16)
    return jnp.dot(hidden, down_mat, preferred_element_type=F32).astype(BF16)


def direct(tokens, ids, scores, w_gate, w_up, w_down):
    rows, picks = ids.shape
    n = lax.axis_size("expert")
    width = tokens.shape[1]
    weights = scores / jnp.sum(scores, axis=1, keepdims=True)
    flat = ids.reshape(-1)
    experts = jnp.arange(n, dtype=jnp.int32)
    member = (flat[:, None] == experts[None, :]).astype(jnp.int32)
    before = jnp.cumsum(member, axis=0) - member
    target = flat * MOST + jnp.sum(before * member, axis=1)
    sent = jnp.zeros((n * MOST, width), BF16).at[target].set(jnp.repeat(tokens, picks, axis=0))
    got = exchange(sent.reshape(n, MOST * LINES, 128))
    served = expert_ffn(got.reshape(n * MOST, width), w_gate[0], w_up[0], w_down[0])
    answered = exchange(served.reshape(n, MOST * LINES, 128)).reshape(n * MOST, width)
    picked = weights.reshape(-1)[:, None] * answered[target].astype(F32)
    return jnp.sum(picked.reshape(rows, picks, width), axis=1).astype(BF16)


def body(tokens, ids, scores, w_gate, w_up, w_down):
    me = lax.axis_index("expert").astype(jnp.int32).reshape(1)
    base, spare, slots, meta = plan(me, ids, tokens)
    mixed = relayed(scores, w_gate, w_up, w_down, base, spare, slots, meta)
    return lax.cond(
        meta[0, 10] == 1,
        lambda mixed, *rest: mixed,
        lambda mixed, *rest: direct(*rest),
        mixed, tokens, ids, scores, w_gate, w_up, w_down,
    )


def solution(mesh):
    placed = (
        P("expert", None),
        P("expert", None),
        P("expert", None),
        P("expert", None, None),
        P("expert", None, None),
        P("expert", None, None),
    )
    return jax.shard_map(
        body, mesh=mesh, in_specs=placed, out_specs=P("expert", None), check_vma=False
    )
```

```python
import functools

import jax
import jax.numpy as jnp
from jax import lax
from jax.experimental import pallas as pl
from jax.experimental.pallas import tpu as pltpu
from jax.sharding import PartitionSpec as P

MOST = 18
BASE = 4
SPARE = 2
CAP = BASE + SPARE
HOT = 3
LINES = 16
DIRS = ((0, 1), (0, -1), (1, 1), (1, -1), (2, 1), (2, -1))
F32 = jnp.float32
BF16 = jnp.bfloat16


def split_index(i):
    return (i >> 5) & 3, (i >> 3) & 3, (i >> 1) & 3


def moved_chip(i, axis, step):
    c = list(split_index(i))
    c[axis] = (c[axis] + step) & 3
    return (c[0] * 4 + c[1]) * 4 + c[2]


def hop_pairs(axis, step, n):
    return [(i, moved_chip(i, axis, step) * 2 + (i & 1)) for i in range(n)]


def plan_kernel(me_ref, ids_ref, tok_ref, out_ref, slot_ref, meta_ref):
    rows, picks = ids_ref.shape
    n = 128
    me = me_ref[0]
    lane = lax.broadcasted_iota(jnp.int32, (1, n), 1)
    lower = (
        lax.broadcasted_iota(jnp.int32, (rows, rows), 1)
        < lax.broadcasted_iota(jnp.int32, (rows, rows), 0)
    ).astype(BF16)
    upper = (
        lax.broadcasted_iota(jnp.int32, (n, n), 0) < lax.broadcasted_iota(jnp.int32, (n, n), 1)
    ).astype(BF16)

    def before_lane(flags):
        wide = jnp.broadcast_to(flags, (8, n)).astype(BF16)
        return jnp.dot(wide, upper, preferred_element_type=F32)[0:1]

    ids = ids_ref[...]
    lane_rows = lax.broadcasted_iota(jnp.int32, (rows, n), 1)
    run = jnp.zeros((1, n), F32)
    ranks, members = [], []
    for k in range(picks):
        member = (ids[:, k : k + 1] == lane_rows).astype(F32)
        ahead = jnp.dot(lower, member.astype(BF16), preferred_element_type=F32) + run
        ranks.append(jnp.sum(ahead * member, axis=1, keepdims=True).astype(jnp.int32))
        members.append(member)
        run = run + jnp.sum(member, axis=0, keepdims=True)
    hot = (run > BASE + 0.5).astype(F32)
    hot_rank = before_lane(hot)

    chips, near, same = [], [], []
    dev = split_index(lane)
    for h in range(HOT):
        mine = hot * (hot_rank == float(h)).astype(F32)
        where_hot = jnp.sum(lane.astype(F32) * mine, axis=1, keepdims=True).astype(jnp.int32)
        chips.append(where_hot >> 1)
        dist = jnp.zeros((1, n), jnp.int32)
        for a, b in zip(dev, split_index(where_hot)):
            gap = (a - b) & 3
            dist = dist + jnp.minimum(gap, 4 - gap)
        same.append((dist == 0).astype(F32))
        near.append((dist == 1).astype(F32))
    taken = jnp.minimum(same[0] + same[1] + same[2], 1.0)
    near = [v * (1.0 - taken) for v in near]
    avail, slot_of, order = [], [], []
    used = jnp.zeros((1, n), F32)
    ok = jnp.ones((1, 1), F32)
    for h in range(HOT):
        free = near[h] * (used < SPARE - 0.5).astype(F32)
        avail.append(free)
        slot_of.append(used)
        order.append(before_lane(free))
        used = used + free
        enough = jnp.sum(free, axis=1, keepdims=True) > MOST - CAP - SPARE - 0.5
        ok = ok * enough.astype(F32)
    for a, b in ((0, 1), (0, 2), (1, 2)):
        ok = ok * (chips[a] != chips[b]).astype(F32)

    wide = lax.broadcasted_iota(jnp.int32, (rows, n * BASE), 1)
    lane_f = lane.astype(F32)
    chosen = [jnp.zeros(wide.shape, F32) for _ in range(3)]
    slot_cols = []
    for k in range(picks):
        e, q, member = ids[:, k : k + 1], ranks[k], members[k]
        which = jnp.sum(member * (hot * (hot_rank + 1.0)), axis=1, keepdims=True)
        code = jnp.where(q < CAP, e * 8 + q, (e ^ 1) * 8 + BASE + (q - CAP))
        far = jnp.zeros((rows, 1), F32)
        turn = (q - (CAP + SPARE)).astype(F32)
        for h in range(HOT):
            hit = avail[h] * (order[h] == turn).astype(F32) * (which == h + 1.0).astype(F32)
            far = far + jnp.sum(hit * (lane_f * 8 + BASE + slot_of[h]), axis=1, keepdims=True)
        code = jnp.where(q < CAP + SPARE, code, far.astype(jnp.int32))
        slot_cols.append(code)
        place, turn = code >> 3, code & 7
        at = jnp.where(turn < BASE, place * BASE + turn, -2)
        half_at = jnp.where(turn < BASE, -2, place * BASE + 2 * (turn - BASE))
        for i, line in enumerate((at, half_at, half_at + 1)):
            chosen[i] = chosen[i] + (line == wide).astype(F32)
    slot_ref[...] = jnp.concatenate(slot_cols, axis=1)
    width = tok_ref.shape[1]
    half = width // 2

    def take(picks_of, first, last):
        return lax.dot_general(
            picks_of.astype(BF16), tok_ref[:, first:last], (((0,), (0,)), ((), ())),
            preferred_element_type=F32,
        )

    out_ref[:, :, :width] = take(chosen[0], 0, width).astype(BF16).reshape(n, BASE, width)
    extra = take(chosen[1], 0, half) + take(chosen[2], half, width)
    out_ref[:, :, width:] = extra.astype(BF16).reshape(n, BASE, half)

    here = (lane == me).astype(F32)
    meta = jnp.zeros((1, n), F32)
    source = [jnp.zeros((1, n), F32) for _ in range(SPARE)]
    for d, (axis, step) in enumerate(DIRS):
        target = moved_chip(lane, axis, step)
        sent = jnp.zeros((1, n), F32)
        for h in range(HOT):
            serves = avail[h] * (target == chips[h]).astype(F32)
            sent = sent + serves * slot_of[h]
            for j in range(SPARE):
                source[j] = source[j] + serves * (slot_of[h] == float(j)).astype(F32) * (1.0 + d)
        meta = jnp.where(lane == d, jnp.sum(sent * here, axis=1, keepdims=True), meta)
    for j in range(SPARE):
        meta = jnp.where(lane == 6 + j, jnp.sum(source[j] * here, axis=1, keepdims=True), meta)
    meta = jnp.where(lane == 8, jnp.sum(hot * here, axis=1, keepdims=True), meta)
    meta = jnp.where(lane == 9, jnp.sum(taken * here, axis=1, keepdims=True), meta)
    meta = jnp.where(lane == 10, ok, meta)
    meta_ref[...] = meta.astype(jnp.int32)


def plan(me, ids, tokens):
    rows, width = tokens.shape
    vmem = pl.BlockSpec(memory_space=pltpu.VMEM)
    return pl.pallas_call(
        plan_kernel,
        in_specs=[pl.BlockSpec(memory_space=pltpu.SMEM), vmem, vmem],
        out_specs=[vmem] * 3,
        out_shape=[
            jax.ShapeDtypeStruct((128, BASE, width * CAP // BASE), BF16),
            jax.ShapeDtypeStruct(ids.shape, jnp.int32),
            jax.ShapeDtypeStruct((1, 128), jnp.int32),
        ],
        compiler_params=pltpu.CompilerParams(vmem_limit_bytes=24 * 2**20),
        name="plan",
    )(me, ids, tokens)


VMEM = pl.BlockSpec(memory_space=pltpu.VMEM)
SMEM = pl.BlockSpec(memory_space=pltpu.SMEM)
HBM = pl.BlockSpec(memory_space=pltpu.HBM)
BLOCK = 256


def spread_kernel(flags_ref, got_ref, *refs):
    outs, parts_ref, sems = refs[:-2], refs[-2], refs[-1]
    n, lines, wide = got_ref.shape
    width = parts_ref.shape[2]
    half = width // 2
    got = got_ref[:, :, width:].reshape(n * lines, half)
    row = lax.broadcasted_iota(jnp.int32, (n, n * lines), 0)
    column = lax.broadcasted_iota(jnp.int32, (n, n * lines), 1)
    for s in range(SPARE):
        for t in range(2):
            take = (row * lines + 2 * s + t == column).astype(BF16)
            part = jnp.dot(take, got, preferred_element_type=F32)
            parts_ref[s, :, t * half : (t + 1) * half] = part.astype(BF16)
    copies = [
        pltpu.make_async_copy(parts_ref.at[i if i < SPARE else flags_ref[i - SPARE]], out, sems.at[i])
        for i, out in enumerate(outs)
    ]
    for copy in copies:
        copy.start()
    for copy in copies:
        copy.wait()


def spread(flags, got):
    n, _, wide = got.shape
    width = wide * BASE // CAP
    count = SPARE + len(DIRS)
    return pl.pallas_call(
        spread_kernel,
        in_specs=[SMEM, VMEM],
        out_specs=[HBM] * count,
        out_shape=[jax.ShapeDtypeStruct((n, width), BF16)] * count,
        scratch_shapes=[pltpu.VMEM((SPARE, n, width), BF16), pltpu.SemaphoreType.DMA((count,))],
        compiler_params=pltpu.CompilerParams(vmem_limit_bytes=24 * 2**20),
        name="spread",
    )(flags, got)


PANEL = 512


def fetcher(choices, scratch):
    hid_ref, gate_ref, up_ref, down_ref, sems = scratch
    blocks = gate_ref.shape[0]

    def copies(weights, i):
        gate, up, down = weights
        if i < blocks:
            at = pl.ds(i * BLOCK, BLOCK)
            pltpu.make_async_copy(gate.at[0, :, at], gate_ref.at[i], sems.at[2 * i]).start()
            pltpu.make_async_copy(up.at[0, :, at], up_ref.at[i], sems.at[2 * i + 1]).start()
        else:
            c = i - blocks
            at = pl.ds(c * PANEL, PANEL)
            pltpu.make_async_copy(down.at[0, :, at], down_ref.at[c], sems.at[2 * blocks + c]).start()

    def start(i):
        for condition, weights in choices:
            if condition is None:
                copies(weights, i)
            else:
                pl.when(condition)(functools.partial(copies, weights, i))

    return start


def ffn_rows(x_ref, out_ref, scratch, start):
    hid_ref, gate_ref, up_ref, down_ref, sems = scratch
    blocks, panels = gate_ref.shape[0], down_ref.shape[0]
    later = list(range(2, blocks + panels))
    per = -(-len(later) // blocks)

    @pl.loop(0, blocks)
    def _(p):
        pltpu.make_async_copy(gate_ref.at[p], gate_ref.at[p], sems.at[2 * p]).wait()
        pltpu.make_async_copy(up_ref.at[p], up_ref.at[p], sems.at[2 * p + 1]).wait()
        for q in range(blocks):
            @pl.when(p == q)
            def _():
                for i in later[q * per : (q + 1) * per]:
                    start(i)

        x = x_ref[...]
        gate_act = jnp.dot(x, gate_ref[p], preferred_element_type=F32)
        upper = jnp.dot(x, up_ref[p], preferred_element_type=F32)
        hid_ref[p] = (jax.nn.silu(gate_act) * upper).astype(BF16)

    @pl.loop(0, panels)
    def _(c):
        pltpu.make_async_copy(down_ref.at[c], down_ref.at[c], sems.at[2 * blocks + c]).wait()
        part = jnp.dot(hid_ref[0], down_ref[c, :BLOCK], preferred_element_type=F32)
        for p in range(1, blocks):
            part += jnp.dot(
                hid_ref[p], down_ref[c, p * BLOCK : (p + 1) * BLOCK], preferred_element_type=F32
            )
        out_ref[:, pl.ds(pl.multiple_of(c * PANEL, PANEL), PANEL)] = part.astype(BF16)


def ffn_scratch(rows, width, inner, more=0):
    blocks, panels = inner // BLOCK, width // PANEL
    return [
        pltpu.VMEM((blocks, rows, BLOCK), BF16),
        pltpu.VMEM((blocks, width, BLOCK), BF16),
        pltpu.VMEM((blocks, width, BLOCK), BF16),
        pltpu.VMEM((panels, inner, PANEL), BF16),
        pltpu.SemaphoreType.DMA((2 * blocks + panels + more,)),
    ]


def ffn_cost(rows, width, inner):
    return pl.CostEstimate(
        flops=6 * rows * width * inner, bytes_accessed=6 * width * inner, transcendentals=0
    )


def ffn_kernel(x_ref, gate, up, down, out_ref, rows_ref, *scratch):
    start = fetcher([(None, (gate, up, down))], scratch)
    start(0)
    start(1)
    rows, width = rows_ref.shape
    rows_ref[...] = x_ref[:, :, :width].reshape(rows, width)
    ffn_rows(rows_ref, out_ref, scratch, start)


def ffn(x, gate_mat, up_mat, down_mat):
    n, slots, _ = x.shape
    width, inner = gate_mat.shape[1:]
    rows = n * slots
    return pl.pallas_call(
        ffn_kernel,
        in_specs=[VMEM] + [HBM] * 3,
        out_specs=VMEM,
        out_shape=jax.ShapeDtypeStruct((rows, width), BF16),
        scratch_shapes=[pltpu.VMEM((rows, width), BF16)] + ffn_scratch(rows, width, inner),
        compiler_params=pltpu.CompilerParams(vmem_limit_bytes=40 * 2**20),
        cost_estimate=ffn_cost(rows, width, inner),
        name="ffn",
    )(x, gate_mat, up_mat, down_mat)


def hot_kernel(groups, flags_ref, *refs):
    xs, refs = refs[:groups], refs[groups:]
    own, other, refs = refs[:3], refs[3:6], refs[6:]
    outs, (rows_ref, done_ref, *scratch) = refs[:groups], refs[groups:]
    n = xs[0].shape[0]
    sems = scratch[-1]
    base = sems.shape[0] - groups

    @pl.when(flags_ref[9] == 1)
    def _():
        parts = [pl.ds(g * n, n) for g in range(groups)]
        arriving = [
            pltpu.make_async_copy(x, rows_ref.at[at], sems.at[base + g])
            for g, (x, at) in enumerate(zip(xs, parts))
        ]
        for copy in arriving:
            copy.start()

        start = fetcher([(flags_ref[8] == 1, own), (flags_ref[8] == 0, other)], scratch)
        start(0)
        start(1)
        for copy in arriving:
            copy.wait()
        ffn_rows(rows_ref, done_ref, scratch, start)
        leaving = [
            pltpu.make_async_copy(done_ref.at[at], out, sems.at[base + g])
            for g, (out, at) in enumerate(zip(outs, parts))
        ]
        for copy in leaving:
            copy.start()
        for copy in leaving:
            copy.wait()


def hot_ffn(flags, xs, own, other):
    n, width = xs[0].shape
    inner = own[0].shape[2]
    rows = n * len(xs)
    return pl.pallas_call(
        functools.partial(hot_kernel, len(xs)),
        in_specs=[SMEM] + [HBM] * (len(xs) + 6),
        out_specs=[HBM] * len(xs),
        out_shape=[jax.ShapeDtypeStruct((n, width), BF16)] * len(xs),
        scratch_shapes=[pltpu.VMEM((rows, width), BF16)] * 2
        + ffn_scratch(rows, width, inner, len(xs)),
        compiler_params=pltpu.CompilerParams(vmem_limit_bytes=60 * 2**20),
        cost_estimate=ffn_cost(rows, width, inner),
        name="hot_ffn",
    )(flags, *xs, *own, *other)


def join_kernel(flags_ref, served_ref, *refs):
    own, back = refs[:SPARE], refs[SPARE : SPARE + len(DIRS)]
    out_ref, pick_ref, sems = refs[SPARE + len(DIRS) :]
    n, lines, _ = out_ref.shape
    width = served_ref.shape[1]
    half = width // 2
    for s in range(SPARE):
        at = pl.ds(2 * s * n, 2 * n)

        @pl.when((flags_ref[6 + s] == 0) & (flags_ref[9] == 0))
        def _():
            pick_ref[at, :] = jnp.zeros((2 * n, half), BF16)

        for d, source in enumerate((own[s],) + back):
            @pl.when((flags_ref[6 + s] == d) & ((d > 0) | (flags_ref[9] == 1)))
            def _():
                copies = [
                    pltpu.make_async_copy(
                        source.at[:, pl.ds(t * half, half)],
                        pick_ref.at[pl.ds((2 * s + t) * n, n)],
                        sems.at[t],
                    )
                    for t in range(2)
                ]
                for copy in copies:
                    copy.start()
                for copy in copies:
                    copy.wait()

    out_ref[:, :, :width] = served_ref[...].reshape(n, lines, width)
    row = lax.broadcasted_iota(jnp.int32, (n * lines, lines * n), 0)
    column = lax.broadcasted_iota(jnp.int32, (n * lines, lines * n), 1)
    put = ((row & (lines - 1)) * n + row // lines == column).astype(BF16)
    placed = jnp.dot(put, pick_ref[...], preferred_element_type=F32)
    out_ref[:, :, width:] = placed.astype(BF16).reshape(n, lines, half)


def join(flags, served, own, back):
    n, width = own[0].shape
    return pl.pallas_call(
        join_kernel,
        in_specs=[SMEM, VMEM] + [HBM] * (SPARE + len(DIRS)),
        out_specs=VMEM,
        out_shape=jax.ShapeDtypeStruct((n, BASE, width * CAP // BASE), BF16),
        scratch_shapes=[pltpu.VMEM((n * BASE, width // 2), BF16), pltpu.SemaphoreType.DMA((2,))],
        compiler_params=pltpu.CompilerParams(vmem_limit_bytes=24 * 2**20),
        name="join",
    )(flags, served, *own, *back)


def mix_kernel(score_ref, slot_ref, ans_ref, out_ref):
    rows, picks = slot_ref.shape
    n, lines, _ = ans_ref.shape
    width = out_ref.shape[1]
    half = width // 2
    scores = score_ref[...]
    weights = scores / jnp.sum(scores, axis=1, keepdims=True)
    slots = slot_ref[...]
    place, turn = slots >> 3, slots & 7
    base = jnp.where(turn < BASE, place * lines + turn, -2)
    spare = jnp.where(turn < BASE, -2, place * lines + 2 * (turn - BASE))

    def spread_weights(at):
        wide = lax.broadcasted_iota(jnp.int32, (rows, n * lines), 1)
        full = jnp.zeros(wide.shape, F32)
        for k in range(picks):
            full = jnp.where(at[:, k : k + 1] == wide, weights[:, k : k + 1], full)
        high = full.astype(BF16)
        low = (full - high.astype(F32)).astype(BF16)
        return jnp.concatenate([high, low], axis=0)

    base_mix = spread_weights(base)
    answers = ans_ref[:, :, :width].reshape(n * lines, width)
    extra = ans_ref[:, :, width:].reshape(n * lines, half)
    for t in range(2):
        at = slice(t * half, (t + 1) * half)
        part = jnp.dot(base_mix, answers[:, at], preferred_element_type=F32)
        part += jnp.dot(spread_weights(spare + t), extra, preferred_element_type=F32)
        out_ref[:, at] = (part[:rows] + part[rows:]).astype(BF16)


def mix(scores, slots, answers):
    n, lines, wide = answers.shape
    return pl.pallas_call(
        mix_kernel,
        in_specs=[VMEM] * 3,
        out_specs=VMEM,
        out_shape=jax.ShapeDtypeStruct((slots.shape[0], wide * BASE // CAP), BF16),
        compiler_params=pltpu.CompilerParams(vmem_limit_bytes=24 * 2**20),
        name="mix",
    )(scores, slots, answers)


def exchange(x):
    return lax.all_to_all(x, "expert", split_axis=0, concat_axis=0, tiled=True)


def relayed(scores, w_gate, w_up, w_down, outgoing, slots, meta):
    n = lax.axis_size("expert")
    flags = meta[0]
    swap = [(i, i ^ 1) for i in range(n)]
    own = (w_gate, w_up, w_down)
    other = [lax.ppermute(w, "expert", swap) for w in own]
    got, *other = lax.optimization_barrier((exchange(outgoing), *other))
    parts = spread(flags, got)
    kept, sent = parts[:SPARE], parts[SPARE:]
    hopped = [
        lax.ppermute(x, "expert", hop_pairs(axis, step, n)) for x, (axis, step) in zip(sent, DIRS)
    ]
    first = hot_ffn(flags, kept, own, other)
    got, first, hopped[0] = lax.optimization_barrier((got, first, hopped[0]))
    served = ffn(got, *own)
    served, early = lax.optimization_barrier((served, hopped[:3]))
    second = hot_ffn(flags, early, own, other)
    third = hot_ffn(flags, hopped[3:], own, other)
    back = [
        lax.ppermute(x, "expert", hop_pairs(axis, -step, n))
        for x, (axis, step) in zip(list(second) + list(third), DIRS)
    ]
    return mix(scores, slots, exchange(join(flags, served, first, back)))


def expert_ffn(rows, gate_mat, up_mat, down_mat):
    gate_act = jnp.dot(rows, gate_mat, preferred_element_type=F32)
    upper = jnp.dot(rows, up_mat, preferred_element_type=F32)
    hidden = (jax.nn.silu(gate_act) * upper).astype(BF16)
    return jnp.dot(hidden, down_mat, preferred_element_type=F32).astype(BF16)


def direct(tokens, ids, scores, w_gate, w_up, w_down):
    rows, picks = ids.shape
    n = lax.axis_size("expert")
    width = tokens.shape[1]
    weights = scores / jnp.sum(scores, axis=1, keepdims=True)
    flat = ids.reshape(-1)
    experts = jnp.arange(n, dtype=jnp.int32)
    member = (flat[:, None] == experts[None, :]).astype(jnp.int32)
    before = jnp.cumsum(member, axis=0) - member
    target = flat * MOST + jnp.sum(before * member, axis=1)
    sent = jnp.zeros((n * MOST, width), BF16).at[target].set(jnp.repeat(tokens, picks, axis=0))
    got = exchange(sent.reshape(n, MOST * LINES, 128))
    served = expert_ffn(got.reshape(n * MOST, width), w_gate[0], w_up[0], w_down[0])
    answered = exchange(served.reshape(n, MOST * LINES, 128)).reshape(n * MOST, width)
    picked = weights.reshape(-1)[:, None] * answered[target].astype(F32)
    return jnp.sum(picked.reshape(rows, picks, width), axis=1).astype(BF16)


def body(tokens, ids, scores, w_gate, w_up, w_down):
    me = lax.axis_index("expert").astype(jnp.int32).reshape(1)
    outgoing, slots, meta = plan(me, ids, tokens)
    mixed = relayed(scores, w_gate, w_up, w_down, outgoing, slots, meta)
    return lax.cond(
        meta[0, 10] == 1,
        lambda mixed, *rest: mixed,
        lambda mixed, *rest: direct(*rest),
        mixed, tokens, ids, scores, w_gate, w_up, w_down,
    )


def solution(mesh):
    placed = (
        P("expert", None),
        P("expert", None),
        P("expert", None),
        P("expert", None, None),
        P("expert", None, None),
        P("expert", None, None),
    )
    return jax.shard_map(
        body, mesh=mesh, in_specs=placed, out_specs=P("expert", None), check_vma=False
    )
```

```python
import functools

import jax
import jax.numpy as jnp
from jax import lax
from jax.experimental import pallas as pl
from jax.experimental.pallas import tpu as pltpu
from jax.sharding import PartitionSpec as P

MOST = 18
BASE = 4
SPARE = 2
CAP = BASE + SPARE
HOT = 3
LINES = 16
DIRS = ((0, 1), (0, -1), (1, 1), (1, -1), (2, 1), (2, -1))
F32 = jnp.float32
BF16 = jnp.bfloat16


def split_index(i):
    return (i >> 5) & 3, (i >> 3) & 3, (i >> 1) & 3


def moved_chip(i, axis, step):
    c = list(split_index(i))
    c[axis] = (c[axis] + step) & 3
    return (c[0] * 4 + c[1]) * 4 + c[2]


def hop_pairs(axis, step, n):
    return [(i, moved_chip(i, axis, step) * 2 + (i & 1)) for i in range(n)]


def plan_kernel(me_ref, ids_ref, tok_ref, out_ref, slot_ref, meta_ref):
    rows, picks = ids_ref.shape
    n = 128
    me = me_ref[0]
    lane = lax.broadcasted_iota(jnp.int32, (1, n), 1)
    lower = (
        lax.broadcasted_iota(jnp.int32, (rows, rows), 1)
        < lax.broadcasted_iota(jnp.int32, (rows, rows), 0)
    ).astype(BF16)
    upper = (
        lax.broadcasted_iota(jnp.int32, (n, n), 0) < lax.broadcasted_iota(jnp.int32, (n, n), 1)
    ).astype(BF16)

    def before_lane(flags):
        wide = jnp.broadcast_to(flags, (8, n)).astype(BF16)
        return jnp.dot(wide, upper, preferred_element_type=F32)[0:1]

    ids = ids_ref[...]
    lane_rows = lax.broadcasted_iota(jnp.int32, (rows, n), 1)
    run = jnp.zeros((1, n), F32)
    ranks, members = [], []
    for k in range(picks):
        member = (ids[:, k : k + 1] == lane_rows).astype(F32)
        ahead = jnp.dot(lower, member.astype(BF16), preferred_element_type=F32) + run
        ranks.append(jnp.sum(ahead * member, axis=1, keepdims=True).astype(jnp.int32))
        members.append(member)
        run = run + jnp.sum(member, axis=0, keepdims=True)
    hot = (run > BASE + 0.5).astype(F32)
    hot_rank = before_lane(hot)

    chips, near, same = [], [], []
    dev = split_index(lane)
    for h in range(HOT):
        mine = hot * (hot_rank == float(h)).astype(F32)
        where_hot = jnp.sum(lane.astype(F32) * mine, axis=1, keepdims=True).astype(jnp.int32)
        chips.append(where_hot >> 1)
        dist = jnp.zeros((1, n), jnp.int32)
        for a, b in zip(dev, split_index(where_hot)):
            gap = (a - b) & 3
            dist = dist + jnp.minimum(gap, 4 - gap)
        same.append((dist == 0).astype(F32))
        near.append((dist == 1).astype(F32))
    taken = jnp.minimum(same[0] + same[1] + same[2], 1.0)
    near = [v * (1.0 - taken) for v in near]
    avail, slot_of, order = [], [], []
    used = jnp.zeros((1, n), F32)
    ok = jnp.ones((1, 1), F32)
    for h in range(HOT):
        free = near[h] * (used < SPARE - 0.5).astype(F32)
        avail.append(free)
        slot_of.append(used)
        order.append(before_lane(free))
        used = used + free
        enough = jnp.sum(free, axis=1, keepdims=True) > MOST - CAP - SPARE - 0.5
        ok = ok * enough.astype(F32)
    for a, b in ((0, 1), (0, 2), (1, 2)):
        ok = ok * (chips[a] != chips[b]).astype(F32)

    wide = lax.broadcasted_iota(jnp.int32, (rows, n * BASE), 1)
    lane_f = lane.astype(F32)
    chosen = [jnp.zeros(wide.shape, F32) for _ in range(3)]
    slot_cols = []
    for k in range(picks):
        e, q, member = ids[:, k : k + 1], ranks[k], members[k]
        which = jnp.sum(member * (hot * (hot_rank + 1.0)), axis=1, keepdims=True)
        code = jnp.where(q < CAP, e * 8 + q, (e ^ 1) * 8 + BASE + (q - CAP))
        far = jnp.zeros((rows, 1), F32)
        turn = (q - (CAP + SPARE)).astype(F32)
        for h in range(HOT):
            hit = avail[h] * (order[h] == turn).astype(F32) * (which == h + 1.0).astype(F32)
            far = far + jnp.sum(hit * (lane_f * 8 + BASE + slot_of[h]), axis=1, keepdims=True)
        code = jnp.where(q < CAP + SPARE, code, far.astype(jnp.int32))
        slot_cols.append(code)
        place, turn = code >> 3, code & 7
        at = jnp.where(turn < BASE, place * BASE + turn, -2)
        half_at = jnp.where(turn < BASE, -2, place * BASE + 2 * (turn - BASE))
        for i, line in enumerate((at, half_at, half_at + 1)):
            chosen[i] = chosen[i] + (line == wide).astype(F32)
    slot_ref[...] = jnp.concatenate(slot_cols, axis=1)
    width = tok_ref.shape[1]
    half = width // 2

    def take(picks_of, first, last):
        return lax.dot_general(
            picks_of.astype(BF16), tok_ref[:, first:last], (((0,), (0,)), ((), ())),
            preferred_element_type=F32,
        )

    out_ref[:, :, :width] = take(chosen[0], 0, width).astype(BF16).reshape(n, BASE, width)
    extra = take(chosen[1], 0, half) + take(chosen[2], half, width)
    out_ref[:, :, width:] = extra.astype(BF16).reshape(n, BASE, half)

    here = (lane == me).astype(F32)
    meta = jnp.zeros((1, n), F32)
    source = [jnp.zeros((1, n), F32) for _ in range(SPARE)]
    for d, (axis, step) in enumerate(DIRS):
        target = moved_chip(lane, axis, step)
        sent = jnp.zeros((1, n), F32)
        for h in range(HOT):
            serves = avail[h] * (target == chips[h]).astype(F32)
            sent = sent + serves * slot_of[h]
            for j in range(SPARE):
                source[j] = source[j] + serves * (slot_of[h] == float(j)).astype(F32) * (1.0 + d)
        meta = jnp.where(lane == d, jnp.sum(sent * here, axis=1, keepdims=True), meta)
    for j in range(SPARE):
        meta = jnp.where(lane == 6 + j, jnp.sum(source[j] * here, axis=1, keepdims=True), meta)
    meta = jnp.where(lane == 8, jnp.sum(hot * here, axis=1, keepdims=True), meta)
    meta = jnp.where(lane == 9, jnp.sum(taken * here, axis=1, keepdims=True), meta)
    meta = jnp.where(lane == 10, ok, meta)
    meta_ref[...] = meta.astype(jnp.int32)


def plan(me, ids, tokens):
    rows, width = tokens.shape
    vmem = pl.BlockSpec(memory_space=pltpu.VMEM)
    return pl.pallas_call(
        plan_kernel,
        in_specs=[pl.BlockSpec(memory_space=pltpu.SMEM), vmem, vmem],
        out_specs=[vmem] * 3,
        out_shape=[
            jax.ShapeDtypeStruct((128, BASE, width * CAP // BASE), BF16),
            jax.ShapeDtypeStruct(ids.shape, jnp.int32),
            jax.ShapeDtypeStruct((1, 128), jnp.int32),
        ],
        compiler_params=pltpu.CompilerParams(vmem_limit_bytes=24 * 2**20),
        name="plan",
    )(me, ids, tokens)


VMEM = pl.BlockSpec(memory_space=pltpu.VMEM)
SMEM = pl.BlockSpec(memory_space=pltpu.SMEM)
HBM = pl.BlockSpec(memory_space=pltpu.HBM)
BLOCK = 256


def spread_kernel(flags_ref, got_ref, *refs):
    outs, parts_ref, sems = refs[:-2], refs[-2], refs[-1]
    n, lines, wide = got_ref.shape
    width = parts_ref.shape[2]
    half = width // 2
    got = got_ref[:, :, width:].reshape(n * lines, half)
    row = lax.broadcasted_iota(jnp.int32, (n, n * lines), 0)
    column = lax.broadcasted_iota(jnp.int32, (n, n * lines), 1)
    for s in range(SPARE):
        for t in range(2):
            take = (row * lines + 2 * s + t == column).astype(BF16)
            part = jnp.dot(take, got, preferred_element_type=F32)
            parts_ref[s, :, t * half : (t + 1) * half] = part.astype(BF16)
    copies = [
        pltpu.make_async_copy(parts_ref.at[i if i < SPARE else flags_ref[i - SPARE]], out, sems.at[i])
        for i, out in enumerate(outs)
    ]
    for copy in copies:
        copy.start()
    for copy in copies:
        copy.wait()


def spread(flags, got):
    n, _, wide = got.shape
    width = wide * BASE // CAP
    count = SPARE + len(DIRS)
    return pl.pallas_call(
        spread_kernel,
        in_specs=[SMEM, VMEM],
        out_specs=[HBM] * count,
        out_shape=[jax.ShapeDtypeStruct((n, width), BF16)] * count,
        scratch_shapes=[pltpu.VMEM((SPARE, n, width), BF16), pltpu.SemaphoreType.DMA((count,))],
        compiler_params=pltpu.CompilerParams(vmem_limit_bytes=24 * 2**20),
        name="spread",
    )(flags, got)


PANEL = 512


def fetcher(choices, scratch):
    hid_ref, gate_ref, up_ref, down_ref, sems = scratch
    blocks = gate_ref.shape[0]

    def copies(weights, i):
        gate, up, down = weights
        if i < blocks:
            at = pl.ds(i * BLOCK, BLOCK)
            pltpu.make_async_copy(gate.at[0, :, at], gate_ref.at[i], sems.at[2 * i]).start()
            pltpu.make_async_copy(up.at[0, :, at], up_ref.at[i], sems.at[2 * i + 1]).start()
        else:
            c = i - blocks
            at = pl.ds(c * PANEL, PANEL)
            pltpu.make_async_copy(down.at[0, :, at], down_ref.at[c], sems.at[2 * blocks + c]).start()

    def start(i):
        for condition, weights in choices:
            if condition is None:
                copies(weights, i)
            else:
                pl.when(condition)(functools.partial(copies, weights, i))

    return start


def ffn_rows(x_ref, out_ref, scratch, start):
    hid_ref, gate_ref, up_ref, down_ref, sems = scratch
    blocks, panels = gate_ref.shape[0], down_ref.shape[0]
    later = list(range(2, blocks + panels))
    per = -(-len(later) // blocks)

    @pl.loop(0, blocks)
    def _(p):
        pltpu.make_async_copy(gate_ref.at[p], gate_ref.at[p], sems.at[2 * p]).wait()
        pltpu.make_async_copy(up_ref.at[p], up_ref.at[p], sems.at[2 * p + 1]).wait()
        for q in range(blocks):
            @pl.when(p == q)
            def _():
                for i in later[q * per : (q + 1) * per]:
                    start(i)

        x = x_ref[...]
        gate_act = jnp.dot(x, gate_ref[p], preferred_element_type=F32)
        upper = jnp.dot(x, up_ref[p], preferred_element_type=F32)
        hid_ref[p] = (jax.nn.silu(gate_act) * upper).astype(BF16)

    @pl.loop(0, panels)
    def _(c):
        pltpu.make_async_copy(down_ref.at[c], down_ref.at[c], sems.at[2 * blocks + c]).wait()
        part = jnp.dot(hid_ref[0], down_ref[c, :BLOCK], preferred_element_type=F32)
        for p in range(1, blocks):
            part += jnp.dot(
                hid_ref[p], down_ref[c, p * BLOCK : (p + 1) * BLOCK], preferred_element_type=F32
            )
        out_ref[:, pl.ds(pl.multiple_of(c * PANEL, PANEL), PANEL)] = part.astype(BF16)


def ffn_scratch(rows, width, inner, more=0):
    blocks, panels = inner // BLOCK, width // PANEL
    return [
        pltpu.VMEM((blocks, rows, BLOCK), BF16),
        pltpu.VMEM((blocks, width, BLOCK), BF16),
        pltpu.VMEM((blocks, width, BLOCK), BF16),
        pltpu.VMEM((panels, inner, PANEL), BF16),
        pltpu.SemaphoreType.DMA((2 * blocks + panels + more,)),
    ]


def ffn_cost(rows, width, inner):
    return pl.CostEstimate(
        flops=6 * rows * width * inner, bytes_accessed=6 * width * inner, transcendentals=0
    )


def ffn_kernel(x_ref, gate, up, down, out_ref, rows_ref, *scratch):
    start = fetcher([(None, (gate, up, down))], scratch)
    start(0)
    start(1)
    rows, width = rows_ref.shape
    rows_ref[...] = x_ref[:, :, :width].reshape(rows, width)
    ffn_rows(rows_ref, out_ref, scratch, start)


def ffn(x, gate_mat, up_mat, down_mat):
    n, slots, _ = x.shape
    width, inner = gate_mat.shape[1:]
    rows = n * slots
    return pl.pallas_call(
        ffn_kernel,
        in_specs=[VMEM] + [HBM] * 3,
        out_specs=VMEM,
        out_shape=jax.ShapeDtypeStruct((rows, width), BF16),
        scratch_shapes=[pltpu.VMEM((rows, width), BF16)] + ffn_scratch(rows, width, inner),
        compiler_params=pltpu.CompilerParams(vmem_limit_bytes=40 * 2**20),
        cost_estimate=ffn_cost(rows, width, inner),
        name="ffn",
    )(x, gate_mat, up_mat, down_mat)


def hot_kernel(groups, flags_ref, *refs):
    xs, refs = refs[:groups], refs[groups:]
    own, other, refs = refs[:3], refs[3:6], refs[6:]
    outs, (rows_ref, done_ref, *scratch) = refs[:groups], refs[groups:]
    n = xs[0].shape[0]
    sems = scratch[-1]
    base = sems.shape[0] - groups

    @pl.when(flags_ref[9] == 1)
    def _():
        parts = [pl.ds(g * n, n) for g in range(groups)]
        arriving = [
            pltpu.make_async_copy(x, rows_ref.at[at], sems.at[base + g])
            for g, (x, at) in enumerate(zip(xs, parts))
        ]
        for copy in arriving:
            copy.start()

        start = fetcher([(flags_ref[8] == 1, own), (flags_ref[8] == 0, other)], scratch)
        start(0)
        start(1)
        for copy in arriving:
            copy.wait()
        ffn_rows(rows_ref, done_ref, scratch, start)
        leaving = [
            pltpu.make_async_copy(done_ref.at[at], out, sems.at[base + g])
            for g, (out, at) in enumerate(zip(outs, parts))
        ]
        for copy in leaving:
            copy.start()
        for copy in leaving:
            copy.wait()


def hot_ffn(flags, xs, own, other):
    n, width = xs[0].shape
    inner = own[0].shape[2]
    rows = n * len(xs)
    return pl.pallas_call(
        functools.partial(hot_kernel, len(xs)),
        in_specs=[SMEM] + [HBM] * (len(xs) + 6),
        out_specs=[HBM] * len(xs),
        out_shape=[jax.ShapeDtypeStruct((n, width), BF16)] * len(xs),
        scratch_shapes=[pltpu.VMEM((rows, width), BF16)] * 2
        + ffn_scratch(rows, width, inner, len(xs)),
        compiler_params=pltpu.CompilerParams(vmem_limit_bytes=60 * 2**20),
        cost_estimate=ffn_cost(rows, width, inner),
        name="hot_ffn",
    )(flags, *xs, *own, *other)


def join_kernel(flags_ref, served_ref, *refs):
    own, back = refs[:SPARE], refs[SPARE : SPARE + len(DIRS)]
    out_ref, pick_ref, sems = refs[SPARE + len(DIRS) :]
    n, lines, _ = out_ref.shape
    width = served_ref.shape[1]
    half = width // 2
    for s in range(SPARE):
        at = pl.ds(2 * s * n, 2 * n)

        @pl.when((flags_ref[6 + s] == 0) & (flags_ref[9] == 0))
        def _():
            pick_ref[at, :] = jnp.zeros((2 * n, half), BF16)

        for d, source in enumerate((own[s],) + back):
            @pl.when((flags_ref[6 + s] == d) & ((d > 0) | (flags_ref[9] == 1)))
            def _():
                copies = [
                    pltpu.make_async_copy(
                        source.at[:, pl.ds(t * half, half)],
                        pick_ref.at[pl.ds((2 * s + t) * n, n)],
                        sems.at[t],
                    )
                    for t in range(2)
                ]
                for copy in copies:
                    copy.start()
                for copy in copies:
                    copy.wait()

    out_ref[:, :, :width] = served_ref[...].reshape(n, lines, width)
    row = lax.broadcasted_iota(jnp.int32, (n * lines, lines * n), 0)
    column = lax.broadcasted_iota(jnp.int32, (n * lines, lines * n), 1)
    put = ((row & (lines - 1)) * n + row // lines == column).astype(BF16)
    placed = jnp.dot(put, pick_ref[...], preferred_element_type=F32)
    out_ref[:, :, width:] = placed.astype(BF16).reshape(n, lines, half)


def join(flags, served, own, back):
    n, width = own[0].shape
    return pl.pallas_call(
        join_kernel,
        in_specs=[SMEM, VMEM] + [HBM] * (SPARE + len(DIRS)),
        out_specs=VMEM,
        out_shape=jax.ShapeDtypeStruct((n, BASE, width * CAP // BASE), BF16),
        scratch_shapes=[pltpu.VMEM((n * BASE, width // 2), BF16), pltpu.SemaphoreType.DMA((2,))],
        compiler_params=pltpu.CompilerParams(vmem_limit_bytes=24 * 2**20),
        name="join",
    )(flags, served, *own, *back)


def mix_kernel(score_ref, slot_ref, ans_ref, out_ref):
    rows, picks = slot_ref.shape
    n, lines, _ = ans_ref.shape
    width = out_ref.shape[1]
    half = width // 2
    scores = score_ref[...]
    weights = scores / jnp.sum(scores, axis=1, keepdims=True)
    slots = slot_ref[...]
    place, turn = slots >> 3, slots & 7
    base = jnp.where(turn < BASE, place * lines + turn, -2)
    spare = jnp.where(turn < BASE, -2, place * lines + 2 * (turn - BASE))

    def spread_weights(at):
        wide = lax.broadcasted_iota(jnp.int32, (rows, n * lines), 1)
        full = jnp.zeros(wide.shape, F32)
        for k in range(picks):
            full = jnp.where(at[:, k : k + 1] == wide, weights[:, k : k + 1], full)
        high = full.astype(BF16)
        low = (full - high.astype(F32)).astype(BF16)
        return jnp.concatenate([high, low], axis=0)

    base_mix = spread_weights(base)
    answers = ans_ref[:, :, :width].reshape(n * lines, width)
    extra = ans_ref[:, :, width:].reshape(n * lines, half)
    for t in range(2):
        at = slice(t * half, (t + 1) * half)
        part = jnp.dot(base_mix, answers[:, at], preferred_element_type=F32)
        part += jnp.dot(spread_weights(spare + t), extra, preferred_element_type=F32)
        out_ref[:, at] = (part[:rows] + part[rows:]).astype(BF16)


def mix(scores, slots, answers):
    n, lines, wide = answers.shape
    return pl.pallas_call(
        mix_kernel,
        in_specs=[VMEM] * 3,
        out_specs=VMEM,
        out_shape=jax.ShapeDtypeStruct((slots.shape[0], wide * BASE // CAP), BF16),
        compiler_params=pltpu.CompilerParams(vmem_limit_bytes=24 * 2**20),
        name="mix",
    )(scores, slots, answers)


def exchange(x):
    return lax.all_to_all(x, "expert", split_axis=0, concat_axis=0, tiled=True)


def relayed(scores, w_gate, w_up, w_down, outgoing, slots, meta):
    n = lax.axis_size("expert")
    flags = meta[0]
    swap = [(i, i ^ 1) for i in range(n)]
    own = (w_gate, w_up, w_down)
    other = [lax.ppermute(w, "expert", swap) for w in own]
    got, *other = lax.optimization_barrier((exchange(outgoing), *other))
    parts = spread(flags, got)
    kept, sent = parts[:SPARE], parts[SPARE:]
    hopped = [
        lax.ppermute(x, "expert", hop_pairs(axis, step, n)) for x, (axis, step) in zip(sent, DIRS)
    ]
    served = ffn(got, *own)
    served, kept, early = lax.optimization_barrier((served, kept, hopped[:2]))
    first = hot_ffn(flags, list(kept) + early, own, other)
    second = hot_ffn(flags, hopped[2:], own, other)
    back = [
        lax.ppermute(x, "expert", hop_pairs(axis, -step, n))
        for x, (axis, step) in zip(list(first[SPARE:]) + list(second), DIRS)
    ]
    return mix(scores, slots, exchange(join(flags, served, first[:SPARE], back)))


def expert_ffn(rows, gate_mat, up_mat, down_mat):
    gate_act = jnp.dot(rows, gate_mat, preferred_element_type=F32)
    upper = jnp.dot(rows, up_mat, preferred_element_type=F32)
    hidden = (jax.nn.silu(gate_act) * upper).astype(BF16)
    return jnp.dot(hidden, down_mat, preferred_element_type=F32).astype(BF16)


def direct(tokens, ids, scores, w_gate, w_up, w_down):
    rows, picks = ids.shape
    n = lax.axis_size("expert")
    width = tokens.shape[1]
    weights = scores / jnp.sum(scores, axis=1, keepdims=True)
    flat = ids.reshape(-1)
    experts = jnp.arange(n, dtype=jnp.int32)
    member = (flat[:, None] == experts[None, :]).astype(jnp.int32)
    before = jnp.cumsum(member, axis=0) - member
    target = flat * MOST + jnp.sum(before * member, axis=1)
    sent = jnp.zeros((n * MOST, width), BF16).at[target].set(jnp.repeat(tokens, picks, axis=0))
    got = exchange(sent.reshape(n, MOST * LINES, 128))
    served = expert_ffn(got.reshape(n * MOST, width), w_gate[0], w_up[0], w_down[0])
    answered = exchange(served.reshape(n, MOST * LINES, 128)).reshape(n * MOST, width)
    picked = weights.reshape(-1)[:, None] * answered[target].astype(F32)
    return jnp.sum(picked.reshape(rows, picks, width), axis=1).astype(BF16)


def body(tokens, ids, scores, w_gate, w_up, w_down):
    me = lax.axis_index("expert").astype(jnp.int32).reshape(1)
    outgoing, slots, meta = plan(me, ids, tokens)
    mixed = relayed(scores, w_gate, w_up, w_down, outgoing, slots, meta)
    return lax.cond(
        meta[0, 10] == 1,
        lambda mixed, *rest: mixed,
        lambda mixed, *rest: direct(*rest),
        mixed, tokens, ids, scores, w_gate, w_up, w_down,
    )


def solution(mesh):
    placed = (
        P("expert", None),
        P("expert", None),
        P("expert", None),
        P("expert", None, None),
        P("expert", None, None),
        P("expert", None, None),
    )
    return jax.shard_map(
        body, mesh=mesh, in_specs=placed, out_specs=P("expert", None), check_vma=False
    )
```

```python
import functools

import jax
import jax.numpy as jnp
from jax import lax
from jax.experimental import pallas as pl
from jax.experimental.pallas import tpu as pltpu
from jax.sharding import PartitionSpec as P

MOST = 18
BASE = 4
SPARE = 2
CAP = BASE + SPARE
HOT = 3
LINES = 16
DIRS = ((0, 1), (0, -1), (1, 1), (1, -1), (2, 1), (2, -1))
F32 = jnp.float32
BF16 = jnp.bfloat16


def split_index(i):
    return (i >> 5) & 3, (i >> 3) & 3, (i >> 1) & 3


def moved_chip(i, axis, step):
    c = list(split_index(i))
    c[axis] = (c[axis] + step) & 3
    return (c[0] * 4 + c[1]) * 4 + c[2]


def hop_pairs(axis, step, n):
    return [(i, moved_chip(i, axis, step) * 2 + (i & 1)) for i in range(n)]


def plan_kernel(me_ref, ids_ref, tok_ref, base_ref, spare_ref, slot_ref, meta_ref):
    rows, picks = ids_ref.shape
    n = 128
    me = me_ref[0]
    lane = lax.broadcasted_iota(jnp.int32, (1, n), 1)
    lower = (
        lax.broadcasted_iota(jnp.int32, (rows, rows), 1)
        < lax.broadcasted_iota(jnp.int32, (rows, rows), 0)
    ).astype(BF16)
    upper = (
        lax.broadcasted_iota(jnp.int32, (n, n), 0) < lax.broadcasted_iota(jnp.int32, (n, n), 1)
    ).astype(BF16)

    def before_lane(flags):
        wide = jnp.broadcast_to(flags, (8, n)).astype(BF16)
        return jnp.dot(wide, upper, preferred_element_type=F32)[0:1]

    ids = ids_ref[...]
    lane_rows = lax.broadcasted_iota(jnp.int32, (rows, n), 1)
    run = jnp.zeros((1, n), F32)
    ranks, members = [], []
    for k in range(picks):
        member = (ids[:, k : k + 1] == lane_rows).astype(F32)
        ahead = jnp.dot(lower, member.astype(BF16), preferred_element_type=F32) + run
        ranks.append(jnp.sum(ahead * member, axis=1, keepdims=True).astype(jnp.int32))
        members.append(member)
        run = run + jnp.sum(member, axis=0, keepdims=True)
    hot = (run > BASE + 0.5).astype(F32)
    hot_rank = before_lane(hot)

    chips, near, same = [], [], []
    dev = split_index(lane)
    for h in range(HOT):
        mine = hot * (hot_rank == float(h)).astype(F32)
        where_hot = jnp.sum(lane.astype(F32) * mine, axis=1, keepdims=True).astype(jnp.int32)
        chips.append(where_hot >> 1)
        dist = jnp.zeros((1, n), jnp.int32)
        for a, b in zip(dev, split_index(where_hot)):
            gap = (a - b) & 3
            dist = dist + jnp.minimum(gap, 4 - gap)
        same.append((dist == 0).astype(F32))
        near.append((dist == 1).astype(F32))
    taken = jnp.minimum(same[0] + same[1] + same[2], 1.0)
    near = [v * (1.0 - taken) for v in near]
    avail, slot_of, order = [], [], []
    used = jnp.zeros((1, n), F32)
    ok = jnp.ones((1, 1), F32)
    for h in range(HOT):
        free = near[h] * (used < SPARE - 0.5).astype(F32)
        avail.append(free)
        slot_of.append(used)
        order.append(before_lane(free))
        used = used + free
        enough = jnp.sum(free, axis=1, keepdims=True) > MOST - CAP - SPARE - 0.5
        ok = ok * enough.astype(F32)
    for a, b in ((0, 1), (0, 2), (1, 2)):
        ok = ok * (chips[a] != chips[b]).astype(F32)

    base_wide = lax.broadcasted_iota(jnp.int32, (rows, n * BASE), 1)
    spare_wide = lax.broadcasted_iota(jnp.int32, (rows, n * SPARE), 1)
    lane_f = lane.astype(F32)
    chosen_base = jnp.zeros(base_wide.shape, F32)
    chosen_spare = jnp.zeros(spare_wide.shape, F32)
    slot_cols = []
    for k in range(picks):
        e, q, member = ids[:, k : k + 1], ranks[k], members[k]
        which = jnp.sum(member * (hot * (hot_rank + 1.0)), axis=1, keepdims=True)
        code = jnp.where(q < CAP, e * 8 + q, (e ^ 1) * 8 + BASE + (q - CAP))
        far = jnp.zeros((rows, 1), F32)
        turn = (q - (CAP + SPARE)).astype(F32)
        for h in range(HOT):
            hit = avail[h] * (order[h] == turn).astype(F32) * (which == h + 1.0).astype(F32)
            far = far + jnp.sum(hit * (lane_f * 8 + BASE + slot_of[h]), axis=1, keepdims=True)
        code = jnp.where(q < CAP + SPARE, code, far.astype(jnp.int32))
        slot_cols.append(code)
        place, turn = code >> 3, code & 7
        at = jnp.where(turn < BASE, place * BASE + turn, -1)
        chosen_base = chosen_base + (at == base_wide).astype(F32)
        at = jnp.where(turn < BASE, -1, place * SPARE + turn - BASE)
        chosen_spare = chosen_spare + (at == spare_wide).astype(F32)
    slot_ref[...] = jnp.concatenate(slot_cols, axis=1)
    for chosen, out_ref in ((chosen_spare, spare_ref), (chosen_base, base_ref)):
        picked = lax.dot_general(
            chosen.astype(BF16), tok_ref[...], (((0,), (0,)), ((), ())),
            preferred_element_type=F32,
        )
        out_ref[...] = picked.astype(BF16).reshape(out_ref.shape)

    here = (lane == me).astype(F32)
    meta = jnp.zeros((1, n), F32)
    source = [jnp.zeros((1, n), F32) for _ in range(SPARE)]
    for d, (axis, step) in enumerate(DIRS):
        target = moved_chip(lane, axis, step)
        sent = jnp.zeros((1, n), F32)
        for h in range(HOT):
            serves = avail[h] * (target == chips[h]).astype(F32)
            sent = sent + serves * slot_of[h]
            for j in range(SPARE):
                source[j] = source[j] + serves * (slot_of[h] == float(j)).astype(F32) * (1.0 + d)
        meta = jnp.where(lane == d, jnp.sum(sent * here, axis=1, keepdims=True), meta)
    for j in range(SPARE):
        meta = jnp.where(lane == 6 + j, jnp.sum(source[j] * here, axis=1, keepdims=True), meta)
    meta = jnp.where(lane == 8, jnp.sum(hot * here, axis=1, keepdims=True), meta)
    meta = jnp.where(lane == 9, jnp.sum(taken * here, axis=1, keepdims=True), meta)
    meta = jnp.where(lane == 10, ok, meta)
    meta_ref[...] = meta.astype(jnp.int32)


def plan(me, ids, tokens):
    rows, width = tokens.shape
    vmem = pl.BlockSpec(memory_space=pltpu.VMEM)
    return pl.pallas_call(
        plan_kernel,
        in_specs=[pl.BlockSpec(memory_space=pltpu.SMEM), vmem, vmem],
        out_specs=[vmem] * 4,
        out_shape=[
            jax.ShapeDtypeStruct((128, BASE, width), BF16),
            jax.ShapeDtypeStruct((128, SPARE, width), BF16),
            jax.ShapeDtypeStruct(ids.shape, jnp.int32),
            jax.ShapeDtypeStruct((1, 128), jnp.int32),
        ],
        compiler_params=pltpu.CompilerParams(vmem_limit_bytes=24 * 2**20),
        name="plan",
    )(me, ids, tokens)


VMEM = pl.BlockSpec(memory_space=pltpu.VMEM)
SMEM = pl.BlockSpec(memory_space=pltpu.SMEM)
HBM = pl.BlockSpec(memory_space=pltpu.HBM)
BLOCK = 256


def spread_kernel(flags_ref, got_ref, *refs):
    outs, parts_ref, sems = refs[:-2], refs[-2], refs[-1]
    n, spare, width = got_ref.shape
    got = got_ref[...].reshape(n * spare, width)
    row = lax.broadcasted_iota(jnp.int32, (n, n * spare), 0)
    column = lax.broadcasted_iota(jnp.int32, (n, n * spare), 1)
    for s in range(SPARE):
        take = (row * spare + s == column).astype(BF16)
        parts_ref[s] = jnp.dot(take, got, preferred_element_type=F32).astype(BF16)
    copies = [
        pltpu.make_async_copy(parts_ref.at[i if i < SPARE else flags_ref[i - SPARE]], out, sems.at[i])
        for i, out in enumerate(outs)
    ]
    for copy in copies:
        copy.start()
    for copy in copies:
        copy.wait()


def spread(flags, got):
    n, spare, width = got.shape
    count = SPARE + len(DIRS)
    return pl.pallas_call(
        spread_kernel,
        in_specs=[SMEM, VMEM],
        out_specs=[HBM] * count,
        out_shape=[jax.ShapeDtypeStruct((n, width), BF16)] * count,
        scratch_shapes=[pltpu.VMEM((SPARE, n, width), BF16), pltpu.SemaphoreType.DMA((count,))],
        compiler_params=pltpu.CompilerParams(vmem_limit_bytes=24 * 2**20),
        name="spread",
    )(flags, got)


PANEL = 512


def fetch(weights, scratch):
    gate, up, down = weights
    hid_ref, gate_ref, up_ref, down_ref, sems = scratch
    blocks, panels = gate_ref.shape[0], down_ref.shape[0]
    for p in range(blocks):
        at = pl.ds(p * BLOCK, BLOCK)
        pltpu.make_async_copy(gate.at[0, :, at], gate_ref.at[p], sems.at[2 * p]).start()
        pltpu.make_async_copy(up.at[0, :, at], up_ref.at[p], sems.at[2 * p + 1]).start()
    for c in range(panels):
        at = pl.ds(c * PANEL, PANEL)
        pltpu.make_async_copy(down.at[0, :, at], down_ref.at[c], sems.at[2 * blocks + c]).start()


def ffn_rows(x_ref, out_ref, scratch):
    hid_ref, gate_ref, up_ref, down_ref, sems = scratch
    blocks, panels = gate_ref.shape[0], down_ref.shape[0]

    @pl.loop(0, blocks)
    def _(p):
        pltpu.make_async_copy(gate_ref.at[p], gate_ref.at[p], sems.at[2 * p]).wait()
        pltpu.make_async_copy(up_ref.at[p], up_ref.at[p], sems.at[2 * p + 1]).wait()
        x = x_ref[...]
        gate_act = jnp.dot(x, gate_ref[p], preferred_element_type=F32)
        upper = jnp.dot(x, up_ref[p], preferred_element_type=F32)
        hid_ref[p] = (jax.nn.silu(gate_act) * upper).astype(BF16)

    @pl.loop(0, panels)
    def _(c):
        pltpu.make_async_copy(down_ref.at[c], down_ref.at[c], sems.at[2 * blocks + c]).wait()
        part = jnp.dot(hid_ref[0], down_ref[c, :BLOCK], preferred_element_type=F32)
        for p in range(1, blocks):
            part += jnp.dot(
                hid_ref[p], down_ref[c, p * BLOCK : (p + 1) * BLOCK], preferred_element_type=F32
            )
        out_ref[:, pl.ds(pl.multiple_of(c * PANEL, PANEL), PANEL)] = part.astype(BF16)


def ffn_scratch(rows, width, inner, more=0):
    blocks, panels = inner // BLOCK, width // PANEL
    return [
        pltpu.VMEM((blocks, rows, BLOCK), BF16),
        pltpu.VMEM((blocks, width, BLOCK), BF16),
        pltpu.VMEM((blocks, width, BLOCK), BF16),
        pltpu.VMEM((panels, inner, PANEL), BF16),
        pltpu.SemaphoreType.DMA((2 * blocks + panels + more,)),
    ]


def ffn_cost(rows, width, inner):
    return pl.CostEstimate(
        flops=6 * rows * width * inner, bytes_accessed=6 * width * inner, transcendentals=0
    )


def ffn_kernel(x_ref, gate, up, down, out_ref, rows_ref, *scratch):
    fetch((gate, up, down), scratch)
    rows_ref[...] = x_ref[...].reshape(rows_ref.shape)
    ffn_rows(rows_ref, out_ref, scratch)


def ffn(x, gate_mat, up_mat, down_mat):
    n, slots, width = x.shape
    inner = gate_mat.shape[2]
    rows = n * slots
    return pl.pallas_call(
        ffn_kernel,
        in_specs=[VMEM] + [HBM] * 3,
        out_specs=VMEM,
        out_shape=jax.ShapeDtypeStruct((rows, width), BF16),
        scratch_shapes=[pltpu.VMEM((rows, width), BF16)] + ffn_scratch(rows, width, inner),
        compiler_params=pltpu.CompilerParams(vmem_limit_bytes=40 * 2**20),
        cost_estimate=ffn_cost(rows, width, inner),
        name="ffn",
    )(x, gate_mat, up_mat, down_mat)


def hot_kernel(groups, flags_ref, *refs):
    xs, refs = refs[:groups], refs[groups:]
    own, other, refs = refs[:3], refs[3:6], refs[6:]
    outs, (rows_ref, done_ref, *scratch) = refs[:groups], refs[groups:]
    n = xs[0].shape[0]
    sems = scratch[-1]
    base = sems.shape[0] - groups

    @pl.when(flags_ref[9] == 1)
    def _():
        parts = [pl.ds(g * n, n) for g in range(groups)]
        arriving = [
            pltpu.make_async_copy(x, rows_ref.at[at], sems.at[base + g])
            for g, (x, at) in enumerate(zip(xs, parts))
        ]
        for copy in arriving:
            copy.start()

        @pl.when(flags_ref[8] == 1)
        def _():
            fetch(own, scratch)

        @pl.when(flags_ref[8] == 0)
        def _():
            fetch(other, scratch)

        for copy in arriving:
            copy.wait()
        ffn_rows(rows_ref, done_ref, scratch)
        leaving = [
            pltpu.make_async_copy(done_ref.at[at], out, sems.at[base + g])
            for g, (out, at) in enumerate(zip(outs, parts))
        ]
        for copy in leaving:
            copy.start()
        for copy in leaving:
            copy.wait()


def hot_ffn(flags, xs, own, other):
    n, width = xs[0].shape
    inner = own[0].shape[2]
    rows = n * len(xs)
    return pl.pallas_call(
        functools.partial(hot_kernel, len(xs)),
        in_specs=[SMEM] + [HBM] * (len(xs) + 6),
        out_specs=[HBM] * len(xs),
        out_shape=[jax.ShapeDtypeStruct((n, width), BF16)] * len(xs),
        scratch_shapes=[pltpu.VMEM((rows, width), BF16)] * 2
        + ffn_scratch(rows, width, inner, len(xs)),
        compiler_params=pltpu.CompilerParams(vmem_limit_bytes=60 * 2**20),
        cost_estimate=ffn_cost(rows, width, inner),
        name="hot_ffn",
    )(flags, *xs, *own, *other)


def join_kernel(flags_ref, served_ref, *refs):
    own, back = refs[:SPARE], refs[SPARE : SPARE + len(DIRS)]
    out_ref, pick_ref, sems = refs[SPARE + len(DIRS) :]
    n, lines, _ = out_ref.shape
    width = served_ref.shape[1]
    half = width // 2
    for s in range(SPARE):
        at = pl.ds(2 * s * n, 2 * n)

        @pl.when((flags_ref[6 + s] == 0) & (flags_ref[9] == 0))
        def _():
            pick_ref[at, :] = jnp.zeros((2 * n, half), BF16)

        for d, source in enumerate((own[s],) + back):
            @pl.when((flags_ref[6 + s] == d) & ((d > 0) | (flags_ref[9] == 1)))
            def _():
                copies = [
                    pltpu.make_async_copy(
                        source.at[:, pl.ds(t * half, half)],
                        pick_ref.at[pl.ds((2 * s + t) * n, n)],
                        sems.at[t],
                    )
                    for t in range(2)
                ]
                for copy in copies:
                    copy.start()
                for copy in copies:
                    copy.wait()

    out_ref[:, :, :width] = served_ref[...].reshape(n, lines, width)
    row = lax.broadcasted_iota(jnp.int32, (n * lines, lines * n), 0)
    column = lax.broadcasted_iota(jnp.int32, (n * lines, lines * n), 1)
    put = ((row & (lines - 1)) * n + row // lines == column).astype(BF16)
    placed = jnp.dot(put, pick_ref[...], preferred_element_type=F32)
    out_ref[:, :, width:] = placed.astype(BF16).reshape(n, lines, half)


def join(flags, served, own, back):
    n, width = own[0].shape
    return pl.pallas_call(
        join_kernel,
        in_specs=[SMEM, VMEM] + [HBM] * (SPARE + len(DIRS)),
        out_specs=VMEM,
        out_shape=jax.ShapeDtypeStruct((n, BASE, width * CAP // BASE), BF16),
        scratch_shapes=[pltpu.VMEM((n * BASE, width // 2), BF16), pltpu.SemaphoreType.DMA((2,))],
        compiler_params=pltpu.CompilerParams(vmem_limit_bytes=24 * 2**20),
        name="join",
    )(flags, served, *own, *back)


def mix_kernel(score_ref, slot_ref, ans_ref, out_ref):
    rows, picks = slot_ref.shape
    n, lines, _ = ans_ref.shape
    width = out_ref.shape[1]
    half = width // 2
    scores = score_ref[...]
    weights = scores / jnp.sum(scores, axis=1, keepdims=True)
    slots = slot_ref[...]
    place, turn = slots >> 3, slots & 7
    base = jnp.where(turn < BASE, place * lines + turn, -2)
    spare = jnp.where(turn < BASE, -2, place * lines + 2 * (turn - BASE))

    def spread_weights(at):
        wide = lax.broadcasted_iota(jnp.int32, (rows, n * lines), 1)
        full = jnp.zeros(wide.shape, F32)
        for k in range(picks):
            full = jnp.where(at[:, k : k + 1] == wide, weights[:, k : k + 1], full)
        high = full.astype(BF16)
        low = (full - high.astype(F32)).astype(BF16)
        return jnp.concatenate([high, low], axis=0)

    base_mix = spread_weights(base)
    answers = ans_ref[:, :, :width].reshape(n * lines, width)
    extra = ans_ref[:, :, width:].reshape(n * lines, half)
    for t in range(2):
        at = slice(t * half, (t + 1) * half)
        part = jnp.dot(base_mix, answers[:, at], preferred_element_type=F32)
        part += jnp.dot(spread_weights(spare + t), extra, preferred_element_type=F32)
        out_ref[:, at] = (part[:rows] + part[rows:]).astype(BF16)


def mix(scores, slots, answers):
    n, lines, wide = answers.shape
    return pl.pallas_call(
        mix_kernel,
        in_specs=[VMEM] * 3,
        out_specs=VMEM,
        out_shape=jax.ShapeDtypeStruct((slots.shape[0], wide * BASE // CAP), BF16),
        compiler_params=pltpu.CompilerParams(vmem_limit_bytes=24 * 2**20),
        name="mix",
    )(scores, slots, answers)


def exchange(x):
    return lax.all_to_all(x, "expert", split_axis=0, concat_axis=0, tiled=True)


def relayed(scores, w_gate, w_up, w_down, base, spare, slots, meta):
    n = lax.axis_size("expert")
    flags = meta[0]
    swap = [(i, i ^ 1) for i in range(n)]
    own = (w_gate, w_up, w_down)
    other = [lax.ppermute(w, "expert", swap) for w in own]
    got_spare, base, *other = lax.optimization_barrier((exchange(spare), base, *other))
    got_base = exchange(base)
    parts = spread(flags, got_spare)
    kept, sent = parts[:SPARE], parts[SPARE:]
    hopped = [
        lax.ppermute(x, "expert", hop_pairs(axis, step, n)) for x, (axis, step) in zip(sent, DIRS)
    ]
    first = hot_ffn(flags, kept, own, other)
    first, early = lax.optimization_barrier((first, hopped[:5]))
    second = hot_ffn(flags, early, own, other)
    third = hot_ffn(flags, hopped[5:], own, other)
    back = [
        lax.ppermute(x, "expert", hop_pairs(axis, -step, n))
        for x, (axis, step) in zip(list(second) + list(third), DIRS)
    ]
    got_base, *_ = lax.optimization_barrier((got_base, *third))
    served = ffn(got_base, *own)
    return mix(scores, slots, exchange(join(flags, served, first, back)))


def expert_ffn(rows, gate_mat, up_mat, down_mat):
    gate_act = jnp.dot(rows, gate_mat, preferred_element_type=F32)
    upper = jnp.dot(rows, up_mat, preferred_element_type=F32)
    hidden = (jax.nn.silu(gate_act) * upper).astype(BF16)
    return jnp.dot(hidden, down_mat, preferred_element_type=F32).astype(BF16)


def direct(tokens, ids, scores, w_gate, w_up, w_down):
    rows, picks = ids.shape
    n = lax.axis_size("expert")
    width = tokens.shape[1]
    weights = scores / jnp.sum(scores, axis=1, keepdims=True)
    flat = ids.reshape(-1)
    experts = jnp.arange(n, dtype=jnp.int32)
    member = (flat[:, None] == experts[None, :]).astype(jnp.int32)
    before = jnp.cumsum(member, axis=0) - member
    target = flat * MOST + jnp.sum(before * member, axis=1)
    sent = jnp.zeros((n * MOST, width), BF16).at[target].set(jnp.repeat(tokens, picks, axis=0))
    got = exchange(sent.reshape(n, MOST * LINES, 128))
    served = expert_ffn(got.reshape(n * MOST, width), w_gate[0], w_up[0], w_down[0])
    answered = exchange(served.reshape(n, MOST * LINES, 128)).reshape(n * MOST, width)
    picked = weights.reshape(-1)[:, None] * answered[target].astype(F32)
    return jnp.sum(picked.reshape(rows, picks, width), axis=1).astype(BF16)


def body(tokens, ids, scores, w_gate, w_up, w_down):
    me = lax.axis_index("expert").astype(jnp.int32).reshape(1)
    base, spare, slots, meta = plan(me, ids, tokens)
    mixed = relayed(scores, w_gate, w_up, w_down, base, spare, slots, meta)
    return lax.cond(
        meta[0, 10] == 1,
        lambda mixed, *rest: mixed,
        lambda mixed, *rest: direct(*rest),
        mixed, tokens, ids, scores, w_gate, w_up, w_down,
    )


def solution(mesh):
    placed = (
        P("expert", None),
        P("expert", None),
        P("expert", None),
        P("expert", None, None),
        P("expert", None, None),
        P("expert", None, None),
    )
    return jax.shard_map(
        body, mesh=mesh, in_specs=placed, out_specs=P("expert", None), check_vma=False
    )
```
